32 devices in a mesh: ga: 2 (over y), gx: 16 (over z, x, core).
Axes of the slice: x: 2, y: 2, z: 4, core: 2. Of those that a mesh axis runs over, the one named last changes fastest.
Arguments:
- fields: bfloat16 [2048, 512, 128], P('gx', 'ga'), parts along dimension 1, may hold values from -6 to 6
- cotangent: bfloat16 [2048, 512, 128], P('gx', 'ga'), parts along dimension 1, may hold values from -6 to 6
- point_weight: bfloat16 [128, 128], replicated, may hold values from -0.5 to 0.5
- mix_weight: bfloat16 [12, 128, 128], replicated, may hold values from -0.5 to 0.5
- bias_vec: bfloat16 [128], replicated, may hold values from -3 to 3
Outputs:
- grad_input: bfloat16 [2048, 512, 128], P('gx', 'ga'), parts along dimension 1
- grad_mix: bfloat16 [24, 128, 128], P('ga'), parts along dimension 0
- grad_point: bfloat16 [256, 128], P('ga'), parts along dimension 0
- grad_bias: bfloat16 [256], P('ga'), parts along dimension 0
The draws below stay inside these ranges and needn't reach their ends.
There are 2 independent parts, one for each index of `ga`. The reference program is written for one: setup_inputs(seed, part) draws one part's arguments, and reference() takes and returns one part's arrays. A program takes and returns all parts, laid end to end along the dimension named above; an argument that names none is the same for every part. Nothing has to cross between parts.
All inputs are finite; a program needn't handle non-finite values.
Results may differ from the reference program's by a relative error of at most 0.012.
Values sent between devices are 32-bit elements; how exact they have to be, the bound alone decides.
No kernel may reach another device: no remote copies, remote signals or barrier semaphores. Data moves between devices by JAX's collectives and lax.ppermute only.
A program may use at most 128 MiB of HBM per device.

```python
import math
import jax
import jax.numpy as jnp
import numpy as np
from jax import lax

NX = 2048
C = 128
LEVELS = 11
NY = 256


def block_scale(key, extent, pieces, smallest, top_value):
    level, own = 1.0, jax.random.fold_in(key, 6)
    for position, shards_of in pieces:
        heights = jnp.exp(jax.random.uniform(jax.random.fold_in(own, position), (shards_of,), jnp.float32, smallest / len(pieces), top_value / len(pieces)))
        level = level * jnp.repeat(heights, extent[position] // shards_of).reshape([-1 if axis == position else 1 for axis in range(len(extent))])
    return level


def noise(key, shape, spread, most, split=(), held_as=jnp.bfloat16):
    values = jax.random.normal(key, shape, jnp.float32) * spread
    if len(split) > 0:
        values = block_scale(key, shape, split, -0.22, 0.18) * values
    return jnp.clip(values, min=-most, max=most).astype(held_as)


def setup_inputs(seed: int = 0, part: int = 0) -> dict:
    keys = jax.random.split(jax.random.key(seed), 6)
    part_keys = jax.random.split(jax.random.fold_in(keys[5], part), 6)
    fields = noise(part_keys[0], (NX, NY, C), 1.0, 6.0, ((0, 16),))
    cotangent = noise(part_keys[1], (NX, NY, C), 1.0, 6.0, ((0, 16),))
    point_weight = noise(keys[2], (C, C), C ** -0.5, 0.5)
    mix_weight = noise(keys[3], (LEVELS + 1, C, C), C ** -0.5, 0.5)
    bias_vec = noise(keys[4], (C,), 0.5, 3.0)
    return dict(fields=fields, cotangent=cotangent, point_weight=point_weight, mix_weight=mix_weight, bias_vec=bias_vec)


root_half = 0.7071067811865476

def haar_forward(signal, depth_count):
    for degree in range(depth_count):
        stride = 2 ** degree
        shaped = signal.reshape((signal.shape[0] // (2 * stride), 2, stride) + signal.shape[1:])
        even_rows = shaped[:, 0, 0]
        odd_rows = shaped[:, 1, 0]
        shaped = shaped.at[:, 0, 0].set((even_rows + odd_rows) * root_half)
        shaped = shaped.at[:, 1, 0].set((odd_rows - even_rows) * root_half)
        signal = shaped.reshape(signal.shape)
    return signal

def haar_inverse(signal, depth_count):
    for degree in reversed(range(depth_count)):
        stride = 2 ** degree
        shaped = signal.reshape((signal.shape[0] // (2 * stride), 2, stride) + signal.shape[1:])
        coarse_rows = shaped[:, 0, 0]
        detail_rows = shaped[:, 1, 0]
        shaped = shaped.at[:, 0, 0].set((coarse_rows - detail_rows) * root_half)
        shaped = shaped.at[:, 1, 0].set((coarse_rows + detail_rows) * root_half)
        signal = shaped.reshape(signal.shape)
    return signal

def mix_levels(coeffs_b, weights, depth_count, first_weight):
    output = jnp.zeros(coeffs_b.shape, jnp.float32)
    for degree in range(depth_count):
        stride = 2 ** degree
        picked = coeffs_b[stride::2 * stride]
        output = output.at[stride::2 * stride].set(jnp.dot(picked, weights[degree], preferred_element_type=jnp.float32))
    output = output.at[0].set(jnp.dot(coeffs_b[0], first_weight, preferred_element_type=jnp.float32))
    return output

def outer_sum(left, right):
    left_flat = left.reshape((-1, left.shape[-1]))
    right_flat = right.reshape((-1, right.shape[-1]))
    return lax.dot_general(left_flat, right_flat, (((0,), (0,)), ((), ())), preferred_element_type=jnp.float32)

def gelu_slope(pre_act, cotangent):
    unused_out, pullback = jax.vjp(jax.nn.gelu, pre_act)
    return pullback(cotangent.astype(pre_act.dtype))[0].astype(jnp.bfloat16)

def level_factors(columns):
    counts = [columns * NX / 2 ** (degree + 1) for degree in range(LEVELS)] + [columns]
    return np.array([1.0 / math.sqrt(value) for value in counts], np.float32)

def reference(fields, cotangent, point_weight, mix_weight, bias_vec):
    coeffs = haar_forward(fields.astype(jnp.float32), LEVELS)
    coeffs_b = coeffs.astype(jnp.bfloat16)
    mixed_rows = mix_levels(coeffs_b, mix_weight, LEVELS, mix_weight[LEVELS])
    spectral = haar_inverse(mixed_rows, LEVELS)
    pre_act = spectral + jnp.dot(fields, point_weight, preferred_element_type=jnp.float32) + bias_vec.astype(jnp.float32)
    slope_b = gelu_slope(pre_act, cotangent)
    back_coeffs = haar_forward(slope_b.astype(jnp.float32), LEVELS)
    back_b = back_coeffs.astype(jnp.bfloat16)
    grads_list = []
    for degree in range(LEVELS):
        stride = 2 ** degree
        grads_list.append(outer_sum(coeffs_b[stride::2 * stride], back_b[stride::2 * stride]))
    grads_list.append(outer_sum(coeffs_b[0:1], back_b[0:1]))
    factors = jnp.asarray(level_factors(fields.shape[1]))
    grad_mix = (jnp.stack(grads_list) * factors[:, None, None]).astype(jnp.bfloat16)
    scale_all = 1.0 / math.sqrt(NX * fields.shape[1])
    grad_point = (outer_sum(fields, slope_b) * scale_all).astype(jnp.bfloat16)
    grad_bias = (lax.optimization_barrier(jnp.sum(slope_b.astype(jnp.float32), axis=(0, 1))) * scale_all).astype(jnp.bfloat16)
    transposed = jnp.swapaxes(mix_weight, 1, 2)
    back_mixed = mix_levels(back_b, transposed, LEVELS, transposed[LEVELS])
    grad_input = (haar_inverse(back_mixed, LEVELS) + jnp.dot(slope_b, point_weight.T, preferred_element_type=jnp.float32)).astype(jnp.bfloat16)
    return (grad_input, grad_mix, grad_point, grad_bias)
```

```python
import functools
import math

import jax
import jax.numpy as jnp
from jax import lax
from jax.experimental import pallas as pl
from jax.experimental.pallas import tpu as pltpu
from jax.sharding import PartitionSpec as P

BF = jnp.bfloat16
F32 = jnp.float32
TILE = 32
GELU_A = math.sqrt(2.0 / math.pi)
GELU_B = 0.044715


def level_starts(depth):
    rows = 1 << depth
    starts, at = [], 0
    for level in range(depth):
        starts.append(at)
        at += rows >> (level + 1)
    return starts


def forward_tree(leaf, put, low, depth, starts):
    if depth == 0:
        return leaf(low)
    half = 1 << (depth - 1)
    even = forward_tree(leaf, put, low, depth - 1, starts)
    odd = forward_tree(leaf, put, low + half, depth - 1, starts)
    put(starts[depth - 1] + (low >> depth), odd - even)
    return even + odd


def inverse_tree(take, leaf, low, depth, starts, value):
    if depth == 0:
        leaf(low, value)
        return
    half = 1 << (depth - 1)
    detail = take(starts[depth - 1] + (low >> depth))
    inverse_tree(take, leaf, low, depth - 1, starts, value - detail)
    inverse_tree(take, leaf, low + half, depth - 1, starts, value + detail)


def mix_details(coeffs_ref, weight_ref, mixed_ref, depth, starts, back):
    columns, channels = coeffs_ref.shape[1:]
    for level in range(depth):
        count = 1 << (depth - 1 - level)
        span = slice(starts[level], starts[level] + count)
        left = coeffs_ref[span].reshape(count * columns, channels)
        dims = (((1,), (1 if back else 0,)), ((), ()))
        mixed = lax.dot_general(left, weight_ref[level], dims, preferred_element_type=F32)
        mixed_ref[span] = mixed.reshape(count, columns, channels)


def kernel_a(depth, fields_ref, weight_ref, coeffs_ref, partial_ref, mixed_ref):
    starts = level_starts(depth)

    def put(row, value):
        coeffs_ref[row] = value.astype(BF)

    forward_tree(lambda row: fields_ref[row].astype(F32), put, 0, depth, starts)
    coeffs_ref[(1 << depth) - 1] = jnp.zeros(coeffs_ref.shape[1:], BF)
    mix_details(coeffs_ref, weight_ref, mixed_ref, depth, starts, False)

    def leaf(row, value):
        partial_ref[row] = value.astype(BF)

    zero = jnp.zeros(mixed_ref.shape[1:], F32)
    inverse_tree(lambda row: mixed_ref[row], leaf, 0, depth, starts, zero)


def kernel_b(depth, partial_ref, cot_ref, base_ref, coeffs_ref, back_ref, coarse_ref, grads_ref):
    starts = level_starts(depth)
    columns, channels = base_ref.shape
    base = base_ref[...]

    def leaf(row):
        v = partial_ref[row].astype(F32) + base
        k = (GELU_A * GELU_B) * (v * v)
        t = jnp.tanh(v * (k + GELU_A))
        w = v * (3.0 * k + GELU_A)
        slope = (0.5 + 0.5 * t) * (1.0 + w * (1.0 - t))
        return (cot_ref[row].astype(F32) * slope).astype(BF).astype(F32)

    def put(row, value):
        back_ref[row] = value.astype(BF)

    coarse_ref[...] = forward_tree(leaf, put, 0, depth, starts)
    back_ref[(1 << depth) - 1] = jnp.zeros((columns, channels), BF)

    @pl.when(pl.program_id(0) == 0)
    def _():
        grads_ref[...] = jnp.zeros_like(grads_ref)

    for level in range(depth):
        count = 1 << (depth - 1 - level)
        span = slice(starts[level], starts[level] + count)
        left = coeffs_ref[span].reshape(count * columns, channels)
        right = back_ref[span].reshape(count * columns, channels)
        grads_ref[level] += lax.dot_general(
            left, right, (((0,), (0,)), ((), ())), preferred_element_type=F32
        )


def kernel_c(depth, back_ref, base_ref, weight_ref, out_ref, mixed_ref):
    starts = level_starts(depth)
    mix_details(back_ref, weight_ref, mixed_ref, depth, starts, True)

    def leaf(row, value):
        out_ref[row] = value.astype(BF)

    inverse_tree(lambda row: mixed_ref[row], leaf, 0, depth, starts, base_ref[...])


def swap(block, stride):
    count = lax.axis_size("gx")
    return lax.ppermute(block, "gx", [(low, low ^ stride) for low in range(count)])


def cross_coeffs(coarse, position, depth):
    found = []
    for degree in range(depth):
        other = swap(coarse, 1 << degree)
        upper = (position >> degree) % 2 == 1
        found.append(jnp.where(upper, coarse - other, other - coarse))
        coarse = coarse + other
    return found + [coarse]


def cross_mix(coeffs_b, weights, position, back):
    spec = "yc,dc->yd" if back else "yc,cd->yd"
    total = jnp.einsum(spec, coeffs_b[-1], weights[-1], preferred_element_type=F32)
    for degree in reversed(range(len(coeffs_b) - 1)):
        upper = (position >> degree) % 2 == 1
        part = jnp.einsum(spec, coeffs_b[degree], weights[degree], preferred_element_type=F32)
        total = total + jnp.where(upper, part, -part)
    return total


def sum_devices(block, position, depth):
    for degree in range(depth):
        half = block.shape[0] // 2
        upper = (position >> degree) % 2 == 1
        low, high = block[:half], block[half:]
        block = jnp.where(upper, high, low) + swap(jnp.where(upper, low, high), 1 << degree)
    for degree in reversed(range(depth)):
        other = swap(block, 1 << degree)
        upper = (position >> degree) % 2 == 1
        block = jnp.where(
            upper, jnp.concatenate([other, block]), jnp.concatenate([block, other])
        )
    return block


def shards(fields, cotangent, point_weight, mix_weight, bias_vec):
    rows, columns, channels = fields.shape
    depth = rows.bit_length() - 1
    device_count = lax.axis_size("gx")
    cross_depth = device_count.bit_length() - 1
    levels = depth + cross_depth
    position = lax.axis_index("gx")
    tile = min(TILE, columns)
    grid = (columns // tile,)
    params = pltpu.CompilerParams(
        dimension_semantics=("arbitrary",), vmem_limit_bytes=48 * 1024 * 1024
    )
    block = pl.BlockSpec((rows, tile, channels), lambda i: (0, i, 0))
    line = pl.BlockSpec((tile, channels), lambda i: (i, 0))
    whole = pl.BlockSpec((depth, channels, channels), lambda i: (0, 0, 0))
    flops = 2 * rows * columns * channels * channels
    moved = 2 * rows * columns * channels

    def cost(passes):
        return pl.CostEstimate(
            flops=flops, bytes_accessed=passes * moved, transcendentals=rows * columns * channels
        )

    powers = [2.0 ** -(level + 1) for level in range(levels)] + [2.0**-levels]
    scale = jnp.array(powers, F32)[:, None, None]
    joined = ((mix_weight.astype(F32) + point_weight.astype(F32)) * scale).astype(BF)

    coarse = jnp.sum(fields.astype(F32), axis=0)
    coeffs_up = [c.astype(BF) for c in cross_coeffs(coarse, position, cross_depth)]
    base = cross_mix(coeffs_up, joined[depth:], position, False) + bias_vec.astype(F32)

    big = jax.ShapeDtypeStruct((rows, columns, channels), BF)
    mixed_scratch = pltpu.VMEM((rows, tile, channels), F32)
    coeffs, partial = pl.pallas_call(
        functools.partial(kernel_a, depth),
        grid=grid,
        in_specs=[block, whole],
        out_specs=[block, block],
        out_shape=[big, big],
        scratch_shapes=[mixed_scratch],
        compiler_params=params,
        cost_estimate=cost(3),
    )(fields, joined[:depth])

    back, slope_coarse, grads = pl.pallas_call(
        functools.partial(kernel_b, depth),
        grid=grid,
        in_specs=[block, block, line, block],
        out_specs=[block, line, whole],
        out_shape=[
            big,
            jax.ShapeDtypeStruct((columns, channels), F32),
            jax.ShapeDtypeStruct((depth, channels, channels), F32),
        ],
        compiler_params=params,
        cost_estimate=cost(4),
    )(partial, cotangent, base, coeffs)

    slope_up = cross_coeffs(slope_coarse, position, cross_depth)
    slope_up_b = [c.astype(BF) for c in slope_up]
    back_base = cross_mix(slope_up_b, joined[depth:], position, True)

    high = slope_coarse.astype(BF)
    low = (slope_coarse - high.astype(F32)).astype(BF)
    outer = functools.partial(jnp.einsum, "yc,yd->cd", preferred_element_type=F32)
    upper_grads = []
    for degree in range(cross_depth - 1):
        part = outer(coeffs_up[degree], high) + outer(coeffs_up[degree], low)
        upper_grads.append(jnp.where((position >> degree) % 2 == 1, part, -part))
    partial_grads = jnp.concatenate([grads] + [g[None] for g in upper_grads])
    summed = sum_devices(partial_grads.reshape(-1, channels), position, cross_depth)
    summed = summed.reshape(-1, channels, channels)
    top = [outer(c, b) for c, b in zip(coeffs_up[-2:], slope_up_b[-2:])]
    raw = jnp.concatenate([summed, jnp.stack(top)]) * scale

    grad_input = pl.pallas_call(
        functools.partial(kernel_c, depth),
        grid=grid,
        in_specs=[block, line, whole],
        out_specs=block,
        out_shape=big,
        scratch_shapes=[mixed_scratch],
        compiler_params=params,
        cost_estimate=cost(2),
    )(back, back_base, joined[:depth])

    global_rows = rows * device_count
    counts = [columns * global_rows / 2 ** (level + 1) for level in range(levels)] + [columns]
    factors = jnp.array([1.0 / math.sqrt(value) for value in counts], F32)
    scale_all = 1.0 / math.sqrt(global_rows * columns)
    grad_mix = (raw * factors[:, None, None]).astype(BF)
    grad_point = (jnp.sum(raw, axis=0) * scale_all).astype(BF)
    grad_bias = (jnp.sum(slope_up[-1], axis=0) * scale_all).astype(BF)
    return (grad_input, grad_mix, grad_point, grad_bias)


def solution(mesh):
    in_specs = (P("gx", "ga", None), P("gx", "ga", None), P(), P(), P())
    out_specs = (P("gx", "ga", None), P("ga", None, None), P("ga", None), P("ga"))
    return jax.shard_map(shards, mesh=mesh, in_specs=in_specs, out_specs=out_specs, check_vma=False)
```

```python
import functools
import math

import jax
import jax.numpy as jnp
from jax import lax
from jax.experimental import pallas as pl
from jax.experimental.pallas import tpu as pltpu
from jax.sharding import PartitionSpec as P

BF = jnp.bfloat16
F32 = jnp.float32
TILE = 32
HBM = pl.BlockSpec(memory_space=pltpu.HBM)
VMEM = pl.BlockSpec(memory_space=pltpu.VMEM)
MIB = 1024 * 1024

GELU_A = math.sqrt(2.0 / math.pi)
GELU_B = 0.044715
STRETCH = math.sqrt(1.5 * GELU_B)
KAPPA = GELU_A * GELU_B / STRETCH**3
UNIT = 1.5 * KAPPA
OFFSET = 1.0 / (3.0 * KAPPA)


def level_starts(depth):
    rows = 1 << depth
    starts, at = [], 0
    for level in range(depth):
        starts.append(at)
        at += rows >> (level + 1)
    return starts


def forward_tree(leaf, put, low, depth, starts):
    half = 1 << (depth - 1)
    row = starts[depth - 1] + (low >> depth)
    if depth == 1:
        even, odd = leaf(low), leaf(low + 1)
        put(0, row, odd - even)
        return even.astype(F32) + odd.astype(F32)
    even = forward_tree(leaf, put, low, depth - 1, starts)
    odd = forward_tree(leaf, put, low + half, depth - 1, starts)
    put(depth - 1, row, (odd - even).astype(BF))
    return even + odd


def inverse_tree(take, leaf, low, depth, starts, value):
    if depth == 0:
        leaf(low, value)
        return
    half = 1 << (depth - 1)
    detail = take(starts[depth - 1] + (low >> depth))
    inverse_tree(take, leaf, low, depth - 1, starts, value - detail)
    inverse_tree(take, leaf, low + half, depth - 1, starts, value + detail)


def mix_details(coeffs_ref, weight_ref, mixed_ref, columns, depth, starts, back):
    tile, channels = mixed_ref.shape[1:]
    for level in range(depth):
        count = 1 << (depth - 1 - level)
        span = slice(starts[level], starts[level] + count)
        left = coeffs_ref[span, columns].reshape(count * tile, channels)
        dims = (((1,), (1 if back else 0,)), ((), ()))
        mixed = lax.dot_general(left, weight_ref[level], dims, preferred_element_type=F32)
        mixed_ref[span] = mixed.reshape(count, tile, channels)


def tile_span(index, tile, first=0):
    return pl.ds(pl.multiple_of(first + index * tile, tile), tile)


def kernel_sum(tile, fields_v, flags_ref, out_ref, flags_out):
    flags_out[...] = flags_ref[...]
    rows, columns = fields_v.shape[:2]

    def step(index, unused):
        here = tile_span(index, tile)
        total = fields_v[0, here].astype(F32)
        for row in range(1, rows):
            total = total + fields_v[row, here].astype(F32)
        out_ref[here] = total
        return 0

    lax.fori_loop(0, columns // tile, step, 0)


def kernel_a(depth, tile, first, stop, fields_v, weight_ref, token_ref, old_c, old_p, coeffs_v, partial_v, mixed_ref):
    starts = level_starts(depth)
    zero = jnp.zeros(mixed_ref.shape[1:], F32)

    def step(index, unused):
        here = tile_span(index, tile, first)

        def put(level, row, value):
            coeffs_v[row, here] = value

        forward_tree(lambda row: fields_v[row, here], put, 0, depth, starts)
        mix_details(coeffs_v, weight_ref, mixed_ref, here, depth, starts, False)

        def leaf(row, value):
            partial_v[row, here] = (value * STRETCH).astype(BF)

        inverse_tree(lambda row: mixed_ref[row], leaf, 0, depth, starts, zero)
        return 0

    lax.fori_loop(0, (stop - first) // tile, step, 0)


def kernel_b(depth, tile, partial_v, cot_v, base_ref, coeffs_v, upper_ref, back_v, coarse_ref, grads_ref):
    starts = level_starts(depth)
    columns, channels = base_ref.shape
    group = max(1, 256 // tile)

    grads_ref[...] = jnp.zeros_like(grads_ref)
    outer = functools.partial(
        lax.dot_general, dimension_numbers=(((0,), (0,)), ((), ())), preferred_element_type=F32
    )

    def step(index, unused):
        here = tile_span(index, tile)
        base = base_ref[here]
        waiting = [[] for _ in range(depth)]

        def leaf(row):
            y = partial_v[row, here].astype(F32) + base
            x = y * (y * y + 1.5)
            t = jnp.tanh(KAPPA * x)
            slope = (1.0 + t) * (OFFSET + (x - y) * (1.0 - t))
            return slope.astype(BF) * cot_v[row, here]

        def put(level, row, value):
            back_v[row, here] = value
            held = waiting[level]
            held.append(value)
            size = len(held)
            if size == group or row + 1 == starts[level] + (1 << (depth - 1 - level)):
                right = jnp.stack(held).reshape(size * tile, channels)
                left = coeffs_v[row + 1 - size : row + 1, here].reshape(size * tile, channels)
                grads_ref[level] += outer(left, right)
                held.clear()

        coarse_ref[here] = forward_tree(leaf, put, 0, depth, starts)
        return 0

    lax.fori_loop(0, columns // tile, step, 0)
    coarse = coarse_ref[...]
    high = coarse.astype(BF)
    low = (coarse - high.astype(F32)).astype(BF)
    for n in range(upper_ref.shape[0]):
        grads_ref[depth + n] = outer(upper_ref[n], high) + outer(upper_ref[n], low)


def kernel_c(depth, tile, first, stop, back_v, base_ref, weight_ref, token_ref, old_out, out_ref, done_ref,
             out_v, mixed_ref, sems):
    starts = level_starts(depth)
    count = (stop - first) // tile
    done_ref[...] = jnp.zeros_like(done_ref)

    def copy(index):
        here = tile_span(index, tile)
        return pltpu.make_async_copy(
            out_v.at[:, here], out_ref.at[:, tile_span(index, tile, first)], sems.at[index]
        )

    def step(index, unused):
        here = tile_span(index, tile)
        there = tile_span(index, tile, first)
        mix_details(back_v, weight_ref, mixed_ref, there, depth, starts, True)

        def leaf(row, value):
            out_v[row, here] = value.astype(BF)

        inverse_tree(lambda row: mixed_ref[row], leaf, 0, depth, starts, base_ref[there])
        copy(index).start()
        return 0

    lax.fori_loop(0, count, step, 0)
    for index in range(count):
        copy(index).wait()


def swap(block, stride):
    count = lax.axis_size("gx")
    return lax.ppermute(block, "gx", [(low, low ^ stride) for low in range(count)])


def is_upper(flags, degree):
    return flags[degree : degree + 1] > 0.5


def cross_coeffs(coarse, flags, depth):
    found, sent = [], []
    for degree in range(depth):
        sent.append(coarse)
        other = swap(coarse, 1 << degree)
        found.append(jnp.where(is_upper(flags, degree), coarse - other, other - coarse))
        coarse = coarse + other
    return found + [coarse], sent


def cross_mix(coeffs_b, weights, flags, back):
    spec = "yc,dc->yd" if back else "yc,cd->yd"
    total = jnp.einsum(spec, coeffs_b[-1], weights[-1], preferred_element_type=F32)
    for degree in reversed(range(len(coeffs_b) - 1)):
        part = jnp.einsum(spec, coeffs_b[degree], weights[degree], preferred_element_type=F32)
        total = total + jnp.where(is_upper(flags, degree), part, -part)
    return total


def sum_devices(block, flags, depth, beside):
    zero = 0
    for degree in range(depth):
        half = block.shape[0] // 2
        upper = is_upper(flags, degree)
        low, high = block[:half], block[half:]
        keep, send = jnp.where(upper, high, low), jnp.where(upper, low, high)
        if degree == depth - 1:
            zero = beside(0, send)
            keep = jnp.where(is_upper(flags + zero, degree), high, low)
        block = keep + swap(send, 1 << degree)
    for degree in reversed(range(depth)):
        other = swap(block, 1 << degree)
        zero = beside(depth - degree, block) if degree else 0
        upper = is_upper(flags + zero, degree)
        block = jnp.where(
            upper, jnp.concatenate([other, block]), jnp.concatenate([block, other])
        )
    return block


def pieces(columns, tile, count):
    tiles = columns // tile
    count = min(count, tiles)
    edges = [tiles * n // count * tile for n in range(count + 1)]
    return list(zip(edges[:-1], edges[1:]))


def shards(fields, cotangent, point_weight, mix_weight, bias_vec):
    rows, columns, channels = fields.shape
    depth = rows.bit_length() - 1
    device_count = lax.axis_size("gx")
    cross_depth = device_count.bit_length() - 1
    levels = depth + cross_depth
    bits = (lax.axis_index("gx") >> jnp.arange(cross_depth, dtype=jnp.int32)) & 1
    flags = jnp.broadcast_to(bits.astype(F32)[:, None], (cross_depth, channels))
    tile = min(TILE, columns)
    tiles = columns // tile

    def params(grant):
        return pltpu.CompilerParams(vmem_limit_bytes=grant * MIB)

    shape = (rows, columns, channels)
    kept = pltpu.VMEM(shape, BF)
    DMA = pltpu.SemaphoreType.DMA
    mixed_scratch = pltpu.VMEM((rows, tile, channels), F32)

    def cost(passes, width, products):
        return pl.CostEstimate(
            flops=2 * products * rows * width * channels * channels,
            bytes_accessed=passes * 2 * rows * width * channels,
            transcendentals=0,
        )

    powers = [2.0 ** -(level + 1) for level in range(levels)] + [2.0**-levels]
    scale = jnp.array(powers, F32)[:, None, None]
    joined_f = (mix_weight.astype(F32) + point_weight.astype(F32)) * scale
    joined = joined_f.astype(BF)
    joined_back = (joined_f * UNIT).astype(BF)

    coarse, flags = pl.pallas_call(
        functools.partial(kernel_sum, tile),
        in_specs=[VMEM, VMEM],
        out_specs=[VMEM] * 2,
        out_shape=[
            jax.ShapeDtypeStruct((columns, channels), F32),
            jax.ShapeDtypeStruct((cross_depth, channels), F32),
        ],
        compiler_params=params(12),
        cost_estimate=cost(1, columns, 0),
    )(fields, flags)
    coeffs_up, sent = cross_coeffs(coarse, flags, cross_depth)
    coeffs_up = [c.astype(BF) for c in coeffs_up]
    base = (cross_mix(coeffs_up, joined[depth:], flags, False) + bias_vec.astype(F32)) * STRETCH

    old = []
    ranges = pieces(columns, tile, max(1, cross_depth - 1))
    for (start, stop), token in zip(ranges, sent[-len(ranges) :]):
        kernel = functools.partial(kernel_a, depth, tile, start, stop)
        if not old:
            kernel = functools.partial(first_call, kernel, 3, 2)
        old = pl.pallas_call(
            kernel,
            in_specs=[VMEM, VMEM, HBM] + [VMEM] * len(old),
            out_specs=[VMEM] * 2,
            out_shape=[kept] * 2,
            input_output_aliases={3: 0, 4: 1} if old else {},
            scratch_shapes=[mixed_scratch],
            compiler_params=params(12),
            cost_estimate=cost(3, stop - start, 1),
        )(fields, joined[:depth], token, *old)
    coeffs, partial = old

    count_up = cross_depth - 1
    upper = jnp.stack([
        jnp.where(is_upper(flags, degree), coeffs_up[degree], -coeffs_up[degree])
        for degree in range(count_up)
    ])
    back, slope_coarse, grads = pl.pallas_call(
        functools.partial(kernel_b, depth, tile),
        in_specs=[VMEM] * 5,
        out_specs=[VMEM] * 3,
        out_shape=[
            kept,
            jax.ShapeDtypeStruct((columns, channels), F32),
            jax.ShapeDtypeStruct((depth + count_up, channels, channels), F32),
        ],
        compiler_params=params(12),
        cost_estimate=cost(4, columns, 1),
    )(partial, cotangent, base, coeffs, upper)

    slope_up, unused_sent = cross_coeffs(slope_coarse, flags, cross_depth)
    slope_up_b = [c.astype(BF) for c in slope_up]
    back_base = cross_mix(slope_up_b, joined_back[depth:], flags, True)

    ranges = pieces(columns, tile, cross_depth)
    results = []

    def beside(n, token):
        if n >= len(ranges):
            return 0
        start, stop = ranges[n]
        kernel = functools.partial(kernel_c, depth, tile, start, stop)
        if not results:
            kernel = functools.partial(first_call, kernel, 4, 1)
        grad_input, zero = pl.pallas_call(
            kernel,
            in_specs=[VMEM, VMEM, VMEM, HBM] + [HBM] * len(results),
            out_specs=[HBM, VMEM],
            out_shape=[jax.ShapeDtypeStruct(shape, BF), jax.ShapeDtypeStruct((1, channels), F32)],
            input_output_aliases={4: 0} if results else {},
            scratch_shapes=[
                pltpu.VMEM((rows, stop - start, channels), BF), mixed_scratch, DMA(((stop - start) // tile,))
            ],
            compiler_params=params(12),
            cost_estimate=cost(2, stop - start, 1),
        )(back, back_base, joined_back[:depth], token, *results)
        results[:] = [grad_input]
        return zero

    summed = sum_devices(grads.reshape(-1, channels), flags, cross_depth, beside)
    grad_input = results[0]
    summed = summed.reshape(-1, channels, channels)
    outer = functools.partial(jnp.einsum, "yc,yd->cd", preferred_element_type=F32)
    top = [outer(c, b) for c, b in zip(coeffs_up[-2:], slope_up_b[-2:])]
    raw = jnp.concatenate([summed, jnp.stack(top)]) * (scale * UNIT)

    global_rows = rows * device_count
    counts = [columns * global_rows / 2 ** (level + 1) for level in range(levels)] + [columns]
    factors = jnp.array([1.0 / math.sqrt(value) for value in counts], F32)
    scale_all = 1.0 / math.sqrt(global_rows * columns)
    grad_mix = (raw * factors[:, None, None]).astype(BF)
    grad_point = (jnp.sum(raw, axis=0) * scale_all).astype(BF)
    grad_bias = (jnp.sum(slope_up[-1], axis=0) * (UNIT * scale_all)).astype(BF)
    return (grad_input, grad_mix, grad_point, grad_bias)


def first_call(kernel, at, count, *refs):
    kernel(*refs[:at], *[None] * count, *refs[at:])


def solution(mesh):
    in_specs = (P("gx", "ga", None), P("gx", "ga", None), P(), P(), P())
    out_specs = (P("gx", "ga", None), P("ga", None, None), P("ga", None), P("ga"))
    return jax.shard_map(shards, mesh=mesh, in_specs=in_specs, out_specs=out_specs, check_vma=False)
```

```python
import functools
import math

import jax
import jax.numpy as jnp
from jax import lax
from jax.experimental import pallas as pl
from jax.experimental.pallas import tpu as pltpu
from jax.sharding import PartitionSpec as P

BF = jnp.bfloat16
F32 = jnp.float32
TILE = 32
HBM = pl.BlockSpec(memory_space=pltpu.HBM)
VMEM = pl.BlockSpec(memory_space=pltpu.VMEM)
MIB = 1024 * 1024

GELU_A = math.sqrt(2.0 / math.pi)
GELU_B = 0.044715
STRETCH = math.sqrt(1.5 * GELU_B)
KAPPA = GELU_A * GELU_B / STRETCH**3
UNIT = 1.5 * KAPPA
OFFSET = 1.0 / (3.0 * KAPPA)


def level_starts(depth):
    rows = 1 << depth
    starts, at = [], 0
    for level in range(depth):
        starts.append(at)
        at += rows >> (level + 1)
    return starts


def forward_tree(leaf, put, low, depth, starts):
    half = 1 << (depth - 1)
    row = starts[depth - 1] + (low >> depth)
    if depth == 1:
        even, odd = leaf(low), leaf(low + 1)
        put(0, row, odd - even)
        return even.astype(F32) + odd.astype(F32)
    even = forward_tree(leaf, put, low, depth - 1, starts)
    odd = forward_tree(leaf, put, low + half, depth - 1, starts)
    put(depth - 1, row, (odd - even).astype(BF))
    return even + odd


def inverse_tree(take, leaf, low, depth, starts, value):
    if depth == 0:
        leaf(low, value)
        return
    half = 1 << (depth - 1)
    detail = take(starts[depth - 1] + (low >> depth))
    inverse_tree(take, leaf, low, depth - 1, starts, value - detail)
    inverse_tree(take, leaf, low + half, depth - 1, starts, value + detail)


def join_weights(mix_ref, point_ref, joined_ref, unit):
    point = point_ref[...].astype(F32)
    for level in range(joined_ref.shape[0]):
        joined_ref[level] = ((mix_ref[level].astype(F32) + point) * (unit * 2.0 ** -(level + 1))).astype(BF)


def mix_details(coeffs_ref, weight_ref, mixed_ref, columns, depth, starts, back):
    tile, channels = mixed_ref.shape[1:]
    for level in range(depth):
        count = 1 << (depth - 1 - level)
        span = slice(starts[level], starts[level] + count)
        left = coeffs_ref[span, columns].reshape(count * tile, channels)
        dims = (((1,), (1 if back else 0,)), ((), ()))
        mixed = lax.dot_general(left, weight_ref[level], dims, preferred_element_type=F32)
        mixed_ref[span] = mixed.reshape(count, tile, channels)


def tile_span(index, tile, first=0):
    return pl.ds(pl.multiple_of(first + index * tile, tile), tile)


def kernel_sum(tile, fields_v, flags_ref, out_ref, flags_out):
    flags_out[...] = flags_ref[...]
    rows, columns = fields_v.shape[:2]

    def step(index, unused):
        here = tile_span(index, tile)
        total = fields_v[0, here].astype(F32)
        for row in range(1, rows):
            total = total + fields_v[row, here].astype(F32)
        out_ref[here] = total
        return 0

    lax.fori_loop(0, columns // tile, step, 0)


def kernel_a(depth, tile, first, stop, fields_v, mix_ref, point_ref, token_ref, old_c, old_p,
             coeffs_v, partial_v, weight_ref, mixed_ref):
    starts = level_starts(depth)
    zero = jnp.zeros(mixed_ref.shape[1:], F32)
    join_weights(mix_ref, point_ref, weight_ref, 1.0)

    def step(index, unused):
        here = tile_span(index, tile, first)

        def put(level, row, value):
            coeffs_v[row, here] = value

        forward_tree(lambda row: fields_v[row, here], put, 0, depth, starts)
        mix_details(coeffs_v, weight_ref, mixed_ref, here, depth, starts, False)

        def leaf(row, value):
            partial_v[row, here] = (value * STRETCH).astype(BF)

        inverse_tree(lambda row: mixed_ref[row], leaf, 0, depth, starts, zero)
        return 0

    lax.fori_loop(0, (stop - first) // tile, step, 0)


def kernel_b(depth, tile, partial_v, cot_v, base_ref, coeffs_v, upper_ref, back_v, coarse_ref, grads_ref):
    starts = level_starts(depth)
    columns, channels = base_ref.shape
    group = max(1, 256 // tile)

    grads_ref[...] = jnp.zeros_like(grads_ref)
    outer = functools.partial(
        lax.dot_general, dimension_numbers=(((0,), (0,)), ((), ())), preferred_element_type=F32
    )

    def step(index, unused):
        here = tile_span(index, tile)
        base = base_ref[here]
        waiting = [[] for _ in range(depth)]

        def leaf(row):
            y = partial_v[row, here].astype(F32) + base
            x = y * (y * y + 1.5)
            t = jnp.tanh(KAPPA * x)
            slope = (1.0 + t) * (OFFSET + (x - y) * (1.0 - t))
            return slope.astype(BF) * cot_v[row, here]

        def put(level, row, value):
            back_v[row, here] = value
            held = waiting[level]
            held.append(value)
            size = len(held)
            if size == group or row + 1 == starts[level] + (1 << (depth - 1 - level)):
                right = jnp.stack(held).reshape(size * tile, channels)
                left = coeffs_v[row + 1 - size : row + 1, here].reshape(size * tile, channels)
                grads_ref[level] += outer(left, right)
                held.clear()

        coarse_ref[here] = forward_tree(leaf, put, 0, depth, starts)
        return 0

    lax.fori_loop(0, columns // tile, step, 0)
    coarse = coarse_ref[...]
    high = coarse.astype(BF)
    low = (coarse - high.astype(F32)).astype(BF)
    for n in range(upper_ref.shape[0]):
        grads_ref[depth + n] = outer(upper_ref[n], high) + outer(upper_ref[n], low)


def kernel_c(depth, tile, first, stop, back_v, base_ref, mix_ref, point_ref, token_ref, old_out, out_ref, done_ref,
             out_v, weight_ref, mixed_ref, sems):
    starts = level_starts(depth)
    count = (stop - first) // tile
    done_ref[...] = jnp.zeros_like(done_ref)
    join_weights(mix_ref, point_ref, weight_ref, UNIT)

    def copy(index):
        here = tile_span(index, tile)
        return pltpu.make_async_copy(
            out_v.at[:, here], out_ref.at[:, tile_span(index, tile, first)], sems.at[index]
        )

    def step(index, unused):
        here = tile_span(index, tile)
        there = tile_span(index, tile, first)
        mix_details(back_v, weight_ref, mixed_ref, there, depth, starts, True)

        def leaf(row, value):
            out_v[row, here] = value.astype(BF)

        inverse_tree(lambda row: mixed_ref[row], leaf, 0, depth, starts, base_ref[there])
        copy(index).start()
        return 0

    lax.fori_loop(0, count, step, 0)
    for index in range(count):
        copy(index).wait()


def swap(block, stride):
    count = lax.axis_size("gx")
    return lax.ppermute(block, "gx", [(low, low ^ stride) for low in range(count)])


def is_upper(flags, degree):
    return flags[degree : degree + 1] > 0.5


def cross_coeffs(coarse, flags, depth):
    found, sent = [], []
    for degree in range(depth):
        sent.append(coarse)
        other = swap(coarse, 1 << degree)
        found.append(jnp.where(is_upper(flags, degree), coarse - other, other - coarse))
        coarse = coarse + other
    return found + [coarse], sent


def mix_row(coeffs_b, weight, back):
    spec = "yc,dc->yd" if back else "yc,cd->yd"
    return jnp.einsum(spec, coeffs_b, weight, preferred_element_type=F32)


def cross_mix(coeffs_b, weights, flags, back, lowest=0):
    total = mix_row(coeffs_b[-1], weights[-1], back)
    for degree in reversed(range(lowest, len(coeffs_b) - 1)):
        part = mix_row(coeffs_b[degree], weights[degree], back)
        total = total + jnp.where(is_upper(flags, degree), part, -part)
    return total


def pick(upper, low, high):
    return jnp.where(upper, high, low), jnp.where(upper, low, high)


def join(upper, mine, other):
    return jnp.where(upper, jnp.concatenate([other, mine]), jnp.concatenate([mine, other]))


def reduce_down(block, coarse, flags, depth):
    found = []
    columns = coarse.shape[0] // 2
    for degree in range(depth):
        upper = is_upper(flags, degree)
        half = block.shape[0] // 2
        keep, send = pick(upper, block[:half], block[half:])
        row_send = coarse
        if degree == 0:
            coarse, row_send = pick(upper, coarse[:columns], coarse[columns:])
        got = swap(jnp.concatenate([send, row_send]), 1 << degree)
        block, other = keep + got[:half], got[half:]
        found.append(jnp.where(upper, coarse - other, other - coarse))
        coarse = coarse + other
    return block, found + [coarse]


def pieces(columns, tile, shares):
    tiles = columns // tile
    total = sum(shares)
    edges = [tiles * sum(shares[:n]) // total * tile for n in range(len(shares) + 1)]
    return [(start, stop) for start, stop in zip(edges[:-1], edges[1:]) if stop > start]


def kernel_last(scales, point_scale, bias_scale, low_ref, high_ref, top_ref, bias_ref, mix_ref, point_ref, out_ref):
    channels = mix_ref.shape[2]
    half = low_ref.shape[0]
    total = jnp.zeros(point_ref.shape, F32)
    for level, (power, factor) in enumerate(scales):
        at = level * channels
        if at + channels <= half:
            raw = low_ref[at : at + channels]
        elif half <= at < 2 * half:
            raw = high_ref[at - half : at - half + channels]
        else:
            raw = top_ref[at - 2 * half : at - 2 * half + channels]
        raw = raw * power
        total = total + raw
        mix_ref[level] = (raw * factor).astype(BF)
    point_ref[...] = (total * point_scale).astype(BF)
    out_ref[...] = (bias_ref[...] * bias_scale).astype(BF)


def shards(fields, cotangent, point_weight, mix_weight, bias_vec):
    rows, columns, channels = fields.shape
    depth = rows.bit_length() - 1
    device_count = lax.axis_size("gx")
    cross_depth = device_count.bit_length() - 1
    levels = depth + cross_depth
    bits = (lax.axis_index("gx") >> jnp.arange(cross_depth, dtype=jnp.int32)) & 1
    flags = jnp.broadcast_to(bits.astype(F32)[:, None], (cross_depth, channels))
    tile = min(TILE, columns)
    tiles = columns // tile

    def params(grant):
        return pltpu.CompilerParams(vmem_limit_bytes=grant * MIB)

    shape = (rows, columns, channels)
    kept = pltpu.VMEM(shape, BF)
    DMA = pltpu.SemaphoreType.DMA
    weight_scratch = pltpu.VMEM((depth, channels, channels), BF)
    mixed_scratch = pltpu.VMEM((rows, tile, channels), F32)

    def cost(passes, width, products):
        return pl.CostEstimate(
            flops=2 * products * rows * width * channels * channels,
            bytes_accessed=passes * 2 * rows * width * channels,
            transcendentals=0,
        )

    powers = [2.0 ** -(level + 1) for level in range(levels)] + [2.0**-levels]
    scale = jnp.array(powers[depth:], F32)[:, None, None]
    joined_f = (mix_weight[depth:].astype(F32) + point_weight.astype(F32)) * scale
    joined = joined_f.astype(BF)
    joined_back = (joined_f * UNIT).astype(BF)

    coarse, flags = pl.pallas_call(
        functools.partial(kernel_sum, tile),
        in_specs=[VMEM, VMEM],
        out_specs=[VMEM] * 2,
        out_shape=[
            jax.ShapeDtypeStruct((columns, channels), F32),
            jax.ShapeDtypeStruct((cross_depth, channels), F32),
        ],
        compiler_params=params(12),
        cost_estimate=cost(1, columns, 0),
    )(fields, flags)
    coeffs_up, sent = cross_coeffs(coarse, flags, cross_depth)
    coeffs_up = [c.astype(BF) for c in coeffs_up]
    base = (cross_mix(coeffs_up, joined, flags, False) + bias_vec.astype(F32)) * STRETCH

    old = []
    ranges = pieces(columns, tile, [1] * max(1, cross_depth - 1))
    for (start, stop), token in zip(ranges, sent[-len(ranges) :]):
        kernel = functools.partial(kernel_a, depth, tile, start, stop)
        if not old:
            kernel = functools.partial(first_call, kernel, 4, 2)
        old = pl.pallas_call(
            kernel,
            in_specs=[VMEM, VMEM, VMEM, HBM] + [VMEM] * len(old),
            out_specs=[VMEM] * 2,
            out_shape=[kept] * 2,
            input_output_aliases={4: 0, 5: 1} if old else {},
            scratch_shapes=[weight_scratch, mixed_scratch],
            compiler_params=params(12),
            cost_estimate=cost(3, stop - start, 1),
        )(fields, mix_weight, point_weight, token, *old)
    coeffs, partial = old

    count_up = cross_depth - 1
    upper = jnp.stack([
        jnp.where(is_upper(flags, degree), coeffs_up[degree], -coeffs_up[degree])
        for degree in range(count_up)
    ])
    back, slope_coarse, grads = pl.pallas_call(
        functools.partial(kernel_b, depth, tile),
        in_specs=[VMEM] * 5,
        out_specs=[VMEM] * 3,
        out_shape=[
            kept,
            jax.ShapeDtypeStruct((columns, channels), F32),
            jax.ShapeDtypeStruct((depth + count_up, channels, channels), F32),
        ],
        compiler_params=params(12),
        cost_estimate=cost(4, columns, 1),
    )(partial, cotangent, base, coeffs, upper)

    block, slope_up = reduce_down(grads.reshape(-1, channels), slope_coarse, flags, cross_depth)
    slope_up_b = [c.astype(BF) for c in slope_up]
    core = is_upper(flags, 0)
    upper_part = cross_mix(slope_up_b, joined_back, flags, True, 1)
    part = mix_row(slope_up_b[0], joined_back[0], True)
    mine, others = pick(core, upper_part - part, upper_part + part)
    back_base = join(core, mine, swap(others, 1))

    ranges = pieces(columns, tile, [3, 4, 1] if cross_depth == 4 else [1] * (cross_depth - 1))
    results = []

    def beside(n, token):
        if n >= len(ranges):
            return 0
        start, stop = ranges[n]
        kernel = functools.partial(kernel_c, depth, tile, start, stop)
        if not results:
            kernel = functools.partial(first_call, kernel, 5, 1)
        grad_input, zero = pl.pallas_call(
            kernel,
            in_specs=[VMEM, VMEM, VMEM, VMEM, HBM] + [HBM] * len(results),
            out_specs=[HBM, VMEM],
            out_shape=[jax.ShapeDtypeStruct(shape, BF), jax.ShapeDtypeStruct((1, channels), F32)],
            input_output_aliases={5: 0} if results else {},
            scratch_shapes=[
                pltpu.VMEM((rows, stop - start, channels), BF), weight_scratch, mixed_scratch, DMA(((stop - start) // tile,))
            ],
            compiler_params=params(12),
            cost_estimate=cost(2, stop - start, 1),
        )(back, back_base, mix_weight, point_weight, token, *results)
        results[:] = [grad_input]
        return zero

    outer = functools.partial(jnp.einsum, "yc,yd->cd", preferred_element_type=F32)
    own_columns = [pick(core, c[: columns // 2], c[columns // 2 :])[0] for c in coeffs_up[-2:]]
    top = jnp.concatenate(
        [outer(c, b) for c, b in zip(own_columns, slope_up_b[-2:])]
        + [jnp.broadcast_to(jnp.sum(slope_up[-1], axis=0, keepdims=True), (8, channels))]
    )
    for degree in reversed(range(1, cross_depth)):
        other = swap(block, 1 << degree)
        zero = beside(cross_depth - 2 - degree, block) if degree < cross_depth - 1 else 0.0
        block = join(is_upper(flags + zero, degree), block, other)
    other = swap(jnp.concatenate([block, top]), 1)
    beside(cross_depth - 2, block)
    half = block.shape[0]
    low, high = jnp.where(core, other[:half], block), jnp.where(core, block, other[:half])
    top = top + other[half:]
    grad_input = results[0]

    global_rows = rows * device_count
    counts = [columns * global_rows / 2 ** (level + 1) for level in range(levels)] + [columns]
    scales = [(power * UNIT, 1.0 / math.sqrt(value)) for power, value in zip(powers, counts)]
    scale_all = 1.0 / math.sqrt(global_rows * columns)
    grad_mix, grad_point, grad_bias = pl.pallas_call(
        functools.partial(kernel_last, scales, scale_all, UNIT * scale_all),
        in_specs=[VMEM] * 4,
        out_specs=[VMEM] * 3,
        out_shape=[
            jax.ShapeDtypeStruct(mix_weight.shape, BF),
            jax.ShapeDtypeStruct(point_weight.shape, BF),
            jax.ShapeDtypeStruct((8, channels), BF),
        ],
        compiler_params=params(12),
    )(low, high, top, top[-8:])
    return (grad_input, grad_mix, grad_point, grad_bias[0])


def first_call(kernel, at, count, *refs):
    kernel(*refs[:at], *[None] * count, *refs[at:])


def solution(mesh):
    in_specs = (P("gx", "ga", None), P("gx", "ga", None), P(), P(), P())
    out_specs = (P("gx", "ga", None), P("ga", None, None), P("ga", None), P("ga"))
    return jax.shard_map(shards, mesh=mesh, in_specs=in_specs, out_specs=out_specs, check_vma=False)
```

```python
import functools
import math

import jax
import jax.numpy as jnp
from jax import lax
from jax.experimental import pallas as pl
from jax.experimental.pallas import tpu as pltpu
from jax.sharding import PartitionSpec as P

BF = jnp.bfloat16
F32 = jnp.float32
TILE = 32
HBM = pl.BlockSpec(memory_space=pltpu.HBM)
VMEM = pl.BlockSpec(memory_space=pltpu.VMEM)
MIB = 1024 * 1024

GELU_A = math.sqrt(2.0 / math.pi)
GELU_B = 0.044715
STRETCH = math.sqrt(1.5 * GELU_B)
KAPPA = GELU_A * GELU_B / STRETCH**3
UNIT = 1.5 * KAPPA
OFFSET = 1.0 / (3.0 * KAPPA)


def level_starts(depth):
    rows = 1 << depth
    starts, at = [], 0
    for level in range(depth):
        starts.append(at)
        at += rows >> (level + 1)
    return starts


def forward_tree(leaf, put, low, depth, starts):
    half = 1 << (depth - 1)
    row = starts[depth - 1] + (low >> depth)
    if depth == 1:
        even, odd = leaf(low), leaf(low + 1)
        put(0, row, odd - even)
        return even.astype(F32) + odd.astype(F32)
    even = forward_tree(leaf, put, low, depth - 1, starts)
    odd = forward_tree(leaf, put, low + half, depth - 1, starts)
    put(depth - 1, row, (odd - even).astype(BF))
    return even + odd


def inverse_tree(take, leaf, low, depth, starts, value):
    if depth == 0:
        leaf(low, value)
        return
    half = 1 << (depth - 1)
    detail = take(starts[depth - 1] + (low >> depth))
    inverse_tree(take, leaf, low, depth - 1, starts, value - detail)
    inverse_tree(take, leaf, low + half, depth - 1, starts, value + detail)


def join_weights(mix_ref, point_ref, joined_ref, unit):
    point = point_ref[...].astype(F32)
    for level in range(joined_ref.shape[0]):
        joined_ref[level] = ((mix_ref[level].astype(F32) + point) * (unit * 2.0 ** -(level + 1))).astype(BF)


def mix_details(coeffs_ref, weight_ref, mixed_ref, columns, depth, starts, back):
    tile, channels = mixed_ref.shape[1:]
    for level in range(depth):
        count = 1 << (depth - 1 - level)
        span = slice(starts[level], starts[level] + count)
        left = coeffs_ref[span, columns].reshape(count * tile, channels)
        dims = (((1,), (1 if back else 0,)), ((), ()))
        mixed = lax.dot_general(left, weight_ref[level], dims, preferred_element_type=F32)
        mixed_ref[span] = mixed.reshape(count, tile, channels)


def tile_span(index, tile, first=0):
    return pl.ds(pl.multiple_of(first + index * tile, tile), tile)


def kernel_sum(tile, fields_v, flags_ref, out_ref, flags_out):
    flags_out[...] = flags_ref[...]
    rows, columns = fields_v.shape[:2]

    def step(index, unused):
        here = tile_span(index, tile)
        total = fields_v[0, here].astype(F32)
        for row in range(1, rows):
            total = total + fields_v[row, here].astype(F32)
        out_ref[here] = total
        return 0

    lax.fori_loop(0, columns // tile, step, 0)


def kernel_a(depth, tile, first, stop, fields_v, mix_ref, point_ref, token_ref, old_c, old_p,
             coeffs_v, partial_v, done_ref, weight_ref, mixed_ref):
    starts = level_starts(depth)
    zero = jnp.zeros(mixed_ref.shape[1:], F32)
    done_ref[...] = jnp.zeros_like(done_ref)
    join_weights(mix_ref, point_ref, weight_ref, 1.0)

    def step(index, unused):
        here = tile_span(index, tile, first)

        def put(level, row, value):
            coeffs_v[row, here] = value

        forward_tree(lambda row: fields_v[row, here], put, 0, depth, starts)
        mix_details(coeffs_v, weight_ref, mixed_ref, here, depth, starts, False)

        def leaf(row, value):
            partial_v[row, here] = (value * STRETCH).astype(BF)

        inverse_tree(lambda row: mixed_ref[row], leaf, 0, depth, starts, zero)
        return 0

    lax.fori_loop(0, (stop - first) // tile, step, 0)


def kernel_b(depth, tile, partial_v, cot_v, base_ref, coeffs_v, upper_ref, back_v, coarse_ref, grads_ref):
    starts = level_starts(depth)
    columns, channels = base_ref.shape
    group = max(1, 256 // tile)

    grads_ref[...] = jnp.zeros_like(grads_ref)
    outer = functools.partial(
        lax.dot_general, dimension_numbers=(((0,), (0,)), ((), ())), preferred_element_type=F32
    )

    def step(index, unused):
        here = tile_span(index, tile)
        base = base_ref[here]
        waiting = [[] for _ in range(depth)]

        def leaf(row):
            y = partial_v[row, here].astype(F32) + base
            x = y * (y * y + 1.5)
            t = jnp.tanh(KAPPA * x)
            slope = (1.0 + t) * (OFFSET + (x - y) * (1.0 - t))
            return slope.astype(BF) * cot_v[row, here]

        def put(level, row, value):
            back_v[row, here] = value
            held = waiting[level]
            held.append(value)
            size = len(held)
            if size == group or row + 1 == starts[level] + (1 << (depth - 1 - level)):
                right = jnp.stack(held).reshape(size * tile, channels)
                left = coeffs_v[row + 1 - size : row + 1, here].reshape(size * tile, channels)
                grads_ref[level] += outer(left, right)
                held.clear()

        coarse_ref[here] = forward_tree(leaf, put, 0, depth, starts)
        return 0

    lax.fori_loop(0, columns // tile, step, 0)
    coarse = coarse_ref[...]
    high = coarse.astype(BF)
    low = (coarse - high.astype(F32)).astype(BF)
    for n in range(upper_ref.shape[0]):
        grads_ref[depth + n] = outer(upper_ref[n], high) + outer(upper_ref[n], low)


def kernel_c(depth, tile, first, stop, back_v, base_ref, mix_ref, point_ref, token_ref, old_out, out_ref, done_ref,
             out_v, weight_ref, mixed_ref, sems):
    starts = level_starts(depth)
    count = (stop - first) // tile
    done_ref[...] = jnp.zeros_like(done_ref)
    join_weights(mix_ref, point_ref, weight_ref, UNIT)

    def copy(index):
        here = tile_span(index, tile)
        return pltpu.make_async_copy(
            out_v.at[:, here], out_ref.at[:, tile_span(index, tile, first)], sems.at[index]
        )

    def step(index, unused):
        here = tile_span(index, tile)
        there = tile_span(index, tile, first)
        mix_details(back_v, weight_ref, mixed_ref, there, depth, starts, True)

        def leaf(row, value):
            out_v[row, here] = value.astype(BF)

        inverse_tree(lambda row: mixed_ref[row], leaf, 0, depth, starts, base_ref[there])
        copy(index).start()
        return 0

    lax.fori_loop(0, count, step, 0)
    for index in range(count):
        copy(index).wait()


def swap(block, stride):
    count = lax.axis_size("gx")
    return lax.ppermute(block, "gx", [(low, low ^ stride) for low in range(count)])


def is_upper(flags, degree):
    return flags[degree : degree + 1] > 0.5


def mix_row(coeffs_b, weight, back):
    spec = "yc,dc->yd" if back else "yc,cd->yd"
    return jnp.einsum(spec, coeffs_b, weight, preferred_element_type=F32)


def cross_mix(coeffs_b, weights, flags, back):
    total = mix_row(coeffs_b[-1], weights[-1], back)
    for degree in reversed(range(1, len(coeffs_b) - 1)):
        part = mix_row(coeffs_b[degree], weights[degree], back)
        total = total + jnp.where(is_upper(flags, degree), part, -part)
    part = mix_row(coeffs_b[0], weights[0], back)
    return pick(is_upper(flags, 0), total - part, total + part)


def pick(upper, low, high):
    return jnp.where(upper, high, low), jnp.where(upper, low, high)


def join(upper, mine, other):
    return jnp.where(upper, jnp.concatenate([other, mine]), jnp.concatenate([mine, other]))


def climb(coarse, flags, depth, block=None, beside=None):
    found = []
    columns = coarse.shape[0] // 2
    for degree in range(depth):
        upper = is_upper(flags, degree)
        send = coarse
        if degree == 0:
            coarse, send = pick(upper, coarse[:columns], coarse[columns:])
        other = half = None
        if block is not None:
            half = block.shape[0] // 2
            keep, gone = pick(upper, block[:half], block[half:])
            send = jnp.concatenate([gone, send])
        other = swap(send, 1 << degree)
        if block is not None:
            block, other = keep + other[:half], other[half:]
        found.append(jnp.where(upper, coarse - other, other - coarse))
        coarse = coarse + other
        if beside is not None:
            coarse = coarse + beside(degree, send)
    return block, found + [coarse]


def pieces(columns, tile, shares):
    tiles = columns // tile
    total = sum(shares)
    edges = [tiles * sum(shares[:n]) // total * tile for n in range(len(shares) + 1)]
    return [(start, stop) for start, stop in zip(edges[:-1], edges[1:]) if stop > start]


def kernel_last(scales, point_scale, bias_scale, low_ref, high_ref, top_ref, mix_ref, point_ref, out_ref):
    channels = mix_ref.shape[2]
    half = low_ref.shape[0]
    total = jnp.zeros(point_ref.shape, F32)
    for level, (power, factor) in enumerate(scales):
        at = level * channels
        if at + channels <= half:
            raw = low_ref[at : at + channels]
        elif half <= at < 2 * half:
            raw = high_ref[at - half : at - half + channels]
        else:
            raw = top_ref[at - 2 * half : at - 2 * half + channels]
        raw = raw * power
        total = total + raw
        mix_ref[level] = (raw * factor).astype(BF)
    point_ref[...] = (total * point_scale).astype(BF)
    out_ref[...] = (top_ref[top_ref.shape[0] - 8 : top_ref.shape[0] - 7] * bias_scale).astype(BF)


def shards(fields, cotangent, point_weight, mix_weight, bias_vec):
    rows, columns, channels = fields.shape
    depth = rows.bit_length() - 1
    device_count = lax.axis_size("gx")
    cross_depth = device_count.bit_length() - 1
    levels = depth + cross_depth
    bits = (lax.axis_index("gx") >> jnp.arange(cross_depth, dtype=jnp.int32)) & 1
    flags = jnp.broadcast_to(bits.astype(F32)[:, None], (cross_depth, channels))
    tile = min(TILE, columns)
    tiles = columns // tile

    def params(grant):
        return pltpu.CompilerParams(vmem_limit_bytes=grant * MIB)

    shape = (rows, columns, channels)
    kept = pltpu.VMEM(shape, BF)
    DMA = pltpu.SemaphoreType.DMA
    weight_scratch = pltpu.VMEM((depth, channels, channels), BF)
    mixed_scratch = pltpu.VMEM((rows, tile, channels), F32)

    def cost(passes, width, products):
        return pl.CostEstimate(
            flops=2 * products * rows * width * channels * channels,
            bytes_accessed=passes * 2 * rows * width * channels,
            transcendentals=0,
        )

    powers = [2.0 ** -(level + 1) for level in range(levels)] + [2.0**-levels]
    scale = jnp.array(powers[depth:], F32)[:, None, None]
    joined_f = (mix_weight[depth:].astype(F32) + point_weight.astype(F32)) * scale
    joined = joined_f.astype(BF)
    joined_back = (joined_f * UNIT).astype(BF)

    coarse, flags = pl.pallas_call(
        functools.partial(kernel_sum, tile),
        in_specs=[VMEM, VMEM],
        out_specs=[VMEM] * 2,
        out_shape=[
            jax.ShapeDtypeStruct((columns, channels), F32),
            jax.ShapeDtypeStruct((cross_depth, channels), F32),
        ],
        compiler_params=params(12),
        cost_estimate=cost(1, columns, 0),
    )(fields, flags)
    core = is_upper(flags, 0)
    count_up = cross_depth - 1
    old = []
    ranges = pieces(columns, tile, [1] * cross_depth)

    def beside_a(n, token):
        if not 0 <= n < len(ranges):
            return 0.0
        start, stop = ranges[n]
        kernel = functools.partial(kernel_a, depth, tile, start, stop)
        if not old:
            kernel = functools.partial(first_call, kernel, 4, 2)
        coeffs, partial, zero = pl.pallas_call(
            kernel,
            in_specs=[VMEM, VMEM, VMEM, HBM] + [VMEM] * len(old),
            out_specs=[VMEM] * 3,
            out_shape=[kept, kept, jax.ShapeDtypeStruct((1, channels), F32)],
            input_output_aliases={4: 0, 5: 1} if old else {},
            scratch_shapes=[weight_scratch, mixed_scratch],
            compiler_params=params(12),
            cost_estimate=cost(3, stop - start, 1),
        )(fields, mix_weight, point_weight, token, *old)
        old[:] = [coeffs, partial]
        return zero

    unused_block, coeffs_up = climb(coarse, flags, cross_depth, None, lambda n, token: beside_a(n - 1, token))
    coeffs_up_b = [c.astype(BF) for c in coeffs_up]
    mine, others = cross_mix(coeffs_up_b, joined, flags, False)
    width = columns // 2
    message = jnp.concatenate([others] + coeffs_up[:count_up])
    got = swap(message, 1)
    beside_a(count_up, message)
    coeffs, partial = old
    base = (join(core, mine, got[:width]) + bias_vec.astype(F32)) * STRETCH
    upper = jnp.stack([
        (join(core, coeffs_up[n], got[(n + 1) * width : (n + 2) * width]) * (2.0 * flags[n : n + 1] - 1.0)).astype(BF)
        for n in range(count_up)
    ])

    back, slope_coarse, grads = pl.pallas_call(
        functools.partial(kernel_b, depth, tile),
        in_specs=[VMEM] * 5,
        out_specs=[VMEM] * 3,
        out_shape=[
            kept,
            jax.ShapeDtypeStruct((columns, channels), F32),
            jax.ShapeDtypeStruct((depth + count_up, channels, channels), F32),
        ],
        compiler_params=params(12),
        cost_estimate=cost(4, columns, 1),
    )(partial, cotangent, base, coeffs, upper)

    block, slope_up = climb(slope_coarse, flags, cross_depth, grads.reshape(-1, channels))
    slope_up_b = [c.astype(BF) for c in slope_up]
    mine, others = cross_mix(slope_up_b, joined_back, flags, True)
    back_base = join(core, mine, swap(others, 1))

    ranges = pieces(columns, tile, [3, 5] if cross_depth == 4 else [1] * (cross_depth - 1))
    results = []

    def beside(n, token):
        if n >= len(ranges):
            return 0
        start, stop = ranges[n]
        kernel = functools.partial(kernel_c, depth, tile, start, stop)
        if not results:
            kernel = functools.partial(first_call, kernel, 5, 1)
        grad_input, zero = pl.pallas_call(
            kernel,
            in_specs=[VMEM, VMEM, VMEM, VMEM, HBM] + [HBM] * len(results),
            out_specs=[HBM, VMEM],
            out_shape=[jax.ShapeDtypeStruct(shape, BF), jax.ShapeDtypeStruct((1, channels), F32)],
            input_output_aliases={5: 0} if results else {},
            scratch_shapes=[
                pltpu.VMEM((rows, stop - start, channels), BF), weight_scratch, mixed_scratch, DMA(((stop - start) // tile,))
            ],
            compiler_params=params(12),
            cost_estimate=cost(2, stop - start, 1),
        )(back, back_base, mix_weight, point_weight, token, *results)
        results[:] = [grad_input]
        return zero

    outer = functools.partial(jnp.einsum, "yc,yd->cd", preferred_element_type=F32)
    top = jnp.concatenate(
        [outer(c, b) for c, b in zip(coeffs_up_b[-2:], slope_up_b[-2:])]
        + [jnp.broadcast_to(jnp.sum(slope_up[-1], axis=0, keepdims=True), (8, channels))]
    )
    for degree in reversed(range(1, cross_depth)):
        other = swap(block, 1 << degree)
        zero = beside(cross_depth - 2 - degree, block) if degree < cross_depth - 1 else 0.0
        block = join(is_upper(flags + zero, degree), block, other)
    other = swap(jnp.concatenate([block, top]), 1)
    beside(cross_depth - 2, block)
    half = block.shape[0]
    low, high = jnp.where(core, other[:half], block), jnp.where(core, block, other[:half])
    top = top + other[half:]
    grad_input = results[0]

    global_rows = rows * device_count
    counts = [columns * global_rows / 2 ** (level + 1) for level in range(levels)] + [columns]
    scales = [(power * UNIT, 1.0 / math.sqrt(value)) for power, value in zip(powers, counts)]
    scale_all = 1.0 / math.sqrt(global_rows * columns)
    grad_mix, grad_point, grad_bias = pl.pallas_call(
        functools.partial(kernel_last, scales, scale_all, UNIT * scale_all),
        in_specs=[VMEM] * 3,
        out_specs=[VMEM] * 3,
        out_shape=[
            jax.ShapeDtypeStruct(mix_weight.shape, BF),
            jax.ShapeDtypeStruct(point_weight.shape, BF),
            jax.ShapeDtypeStruct((1, channels), BF),
        ],
        compiler_params=params(12),
    )(low, high, top)
    return (grad_input, grad_mix, grad_point, grad_bias.reshape(channels))


def first_call(kernel, at, count, *refs):
    kernel(*refs[:at], *[None] * count, *refs[at:])


def solution(mesh):
    in_specs = (P("gx", "ga", None), P("gx", "ga", None), P(), P(), P())
    out_specs = (P("gx", "ga", None), P("ga", None, None), P("ga", None), P("ga"))
    return jax.shard_map(shards, mesh=mesh, in_specs=in_specs, out_specs=out_specs, check_vma=False)
```

```python
import functools
import math

import jax
import jax.numpy as jnp
from jax import lax
from jax.experimental import pallas as pl
from jax.experimental.pallas import tpu as pltpu
from jax.sharding import PartitionSpec as P

BF = jnp.bfloat16
F32 = jnp.float32
TILE = 32
WIDE = 64
HBM = pl.BlockSpec(memory_space=pltpu.HBM)
VMEM = pl.BlockSpec(memory_space=pltpu.VMEM)
MIB = 1024 * 1024

GELU_A = math.sqrt(2.0 / math.pi)
GELU_B = 0.044715
STRETCH = math.sqrt(1.5 * GELU_B)
KAPPA = GELU_A * GELU_B / STRETCH**3
UNIT = 1.5 * KAPPA
OFFSET = 1.0 / (3.0 * KAPPA)


def level_starts(depth):
    rows = 1 << depth
    starts, at = [], 0
    for level in range(depth):
        starts.append(at)
        at += rows >> (level + 1)
    return starts


def forward_tree(leaf, put, low, depth, starts):
    half = 1 << (depth - 1)
    row = starts[depth - 1] + (low >> depth)
    if depth == 1:
        even, odd = leaf(low), leaf(low + 1)
        put(0, row, odd - even)
        return even.astype(F32) + odd.astype(F32)
    even = forward_tree(leaf, put, low, depth - 1, starts)
    odd = forward_tree(leaf, put, low + half, depth - 1, starts)
    put(depth - 1, row, (odd - even).astype(BF))
    return even + odd


def inverse_tree(take, leaf, low, depth, starts, value):
    if depth == 0:
        leaf(low, value)
        return
    half = 1 << (depth - 1)
    detail = take(starts[depth - 1] + (low >> depth))
    inverse_tree(take, leaf, low, depth - 1, starts, value - detail)
    inverse_tree(take, leaf, low + half, depth - 1, starts, value + detail)


def join_weights(mix_ref, point_ref, joined_ref, unit):
    point = point_ref[...].astype(F32)
    for level in range(joined_ref.shape[0]):
        joined_ref[level] = ((mix_ref[level].astype(F32) + point) * (unit * 2.0 ** -(level + 1))).astype(BF)


def mix_details(coeffs_ref, weight_ref, mixed_ref, columns, depth, starts, back):
    tile, channels = mixed_ref.shape[1:]
    for level in range(depth):
        count = 1 << (depth - 1 - level)
        span = slice(starts[level], starts[level] + count)
        left = coeffs_ref[span, columns].reshape(count * tile, channels)
        dims = (((1,), (1 if back else 0,)), ((), ()))
        mixed = lax.dot_general(left, weight_ref[level], dims, preferred_element_type=F32)
        mixed_ref[span] = mixed.reshape(count, tile, channels)


def tile_span(index, tile, first=0):
    return pl.ds(pl.multiple_of(first + index * tile, tile), tile)


def kernel_sum(tile, fields_v, flags_ref, out_ref, flags_out):
    flags_out[...] = flags_ref[...]
    rows, columns = fields_v.shape[:2]

    def step(index, unused):
        here = tile_span(index, tile)
        total = fields_v[0, here].astype(F32)
        for row in range(1, rows):
            total = total + fields_v[row, here].astype(F32)
        out_ref[here] = total
        return 0

    lax.fori_loop(0, columns // tile, step, 0)


def kernel_a(depth, tile, first, stop, fields_v, mix_ref, point_ref, token_ref, old_c, old_p,
             coeffs_v, partial_v, done_ref, weight_ref, mixed_ref):
    starts = level_starts(depth)
    zero = jnp.zeros(mixed_ref.shape[1:], F32)
    done_ref[...] = jnp.zeros_like(done_ref)
    join_weights(mix_ref, point_ref, weight_ref, 1.0)

    def step(index, unused):
        here = tile_span(index, tile, first)

        def put(level, row, value):
            coeffs_v[row, here] = value

        forward_tree(lambda row: fields_v[row, here], put, 0, depth, starts)
        mix_details(coeffs_v, weight_ref, mixed_ref, here, depth, starts, False)

        def leaf(row, value):
            partial_v[row, here] = (value * STRETCH).astype(BF)

        inverse_tree(lambda row: mixed_ref[row], leaf, 0, depth, starts, zero)
        return 0

    lax.fori_loop(0, (stop - first) // tile, step, 0)


def kernel_b(depth, tile, partial_v, cot_v, base_ref, coeffs_v, upper_ref, back_v, coarse_ref, grads_ref):
    starts = level_starts(depth)
    columns, channels = base_ref.shape
    group = max(1, 256 // tile)

    grads_ref[...] = jnp.zeros_like(grads_ref)
    outer = functools.partial(
        lax.dot_general, dimension_numbers=(((0,), (0,)), ((), ())), preferred_element_type=F32
    )

    def step(index, unused):
        here = tile_span(index, tile)
        base = base_ref[here]
        waiting = [[] for _ in range(depth)]

        def leaf(row):
            y = partial_v[row, here].astype(F32) + base
            x = y * (y * y + 1.5)
            t = jnp.tanh(KAPPA * x)
            slope = (1.0 + t) * (OFFSET + (x - y) * (1.0 - t))
            return slope.astype(BF) * cot_v[row, here]

        def put(level, row, value):
            back_v[row, here] = value
            held = waiting[level]
            held.append(value)
            size = len(held)
            if size == group or row + 1 == starts[level] + (1 << (depth - 1 - level)):
                right = jnp.stack(held).reshape(size * tile, channels)
                left = coeffs_v[row + 1 - size : row + 1, here].reshape(size * tile, channels)
                grads_ref[level] += outer(left, right)
                held.clear()

        coarse_ref[here] = forward_tree(leaf, put, 0, depth, starts)
        return 0

    lax.fori_loop(0, columns // tile, step, 0)
    coarse = coarse_ref[...]
    high = coarse.astype(BF)
    low = (coarse - high.astype(F32)).astype(BF)
    for n in range(upper_ref.shape[0]):
        grads_ref[depth + n] = outer(upper_ref[n], high) + outer(upper_ref[n], low)


def kernel_c(depth, tile, first, stop, back_v, base_ref, mix_ref, point_ref, token_ref, old_out, out_ref, done_ref,
             out_v, weight_ref, mixed_ref, sems):
    starts = level_starts(depth)
    count = (stop - first) // tile
    done_ref[...] = jnp.zeros_like(done_ref)
    join_weights(mix_ref, point_ref, weight_ref, UNIT)

    def copy(index):
        here = tile_span(index, tile)
        return pltpu.make_async_copy(
            out_v.at[:, here], out_ref.at[:, tile_span(index, tile, first)], sems.at[index]
        )

    def step(index, unused):
        here = tile_span(index, tile)
        there = tile_span(index, tile, first)
        mix_details(back_v, weight_ref, mixed_ref, there, depth, starts, True)

        def leaf(row, value):
            out_v[row, here] = value.astype(BF)

        inverse_tree(lambda row: mixed_ref[row], leaf, 0, depth, starts, base_ref[there])
        copy(index).start()
        return 0

    lax.fori_loop(0, count, step, 0)
    for index in range(count):
        copy(index).wait()


def swap(block, stride):
    count = lax.axis_size("gx")
    return lax.ppermute(block, "gx", [(low, low ^ stride) for low in range(count)])


def is_upper(flags, degree):
    return flags[degree : degree + 1] > 0.5


def mix_row(coeffs_b, weight, back):
    spec = "yc,dc->yd" if back else "yc,cd->yd"
    return jnp.einsum(spec, coeffs_b, weight, preferred_element_type=F32)


def cross_mix(coeffs_b, weights, flags, back):
    total = mix_row(coeffs_b[-1], weights[-1], back)
    for degree in reversed(range(1, len(coeffs_b) - 1)):
        part = mix_row(coeffs_b[degree], weights[degree], back)
        total = total + jnp.where(is_upper(flags, degree), part, -part)
    part = mix_row(coeffs_b[0], weights[0], back)
    return pick(is_upper(flags, 0), total - part, total + part)


def pick(upper, low, high):
    return jnp.where(upper, high, low), jnp.where(upper, low, high)


def join(upper, mine, other):
    return jnp.where(upper, jnp.concatenate([other, mine]), jnp.concatenate([mine, other]))


def climb(coarse, flags, depth, block=None, beside=None):
    found = []
    columns = coarse.shape[0] // 2
    for degree in range(depth):
        upper = is_upper(flags, degree)
        send = coarse
        if degree == 0:
            coarse, send = pick(upper, coarse[:columns], coarse[columns:])
        other = half = None
        if block is not None:
            half = block.shape[0] // 2
            keep, gone = pick(upper, block[:half], block[half:])
            send = jnp.concatenate([gone, send])
        other = swap(send, 1 << degree)
        if block is not None:
            block, other = keep + other[:half], other[half:]
        found.append(jnp.where(upper, coarse - other, other - coarse))
        coarse = coarse + other
        if beside is not None:
            coarse = coarse + beside(degree, send)
    return block, found + [coarse]


def pieces(columns, tile, shares):
    tiles = columns // tile
    total = sum(shares)
    edges = [tiles * sum(shares[:n]) // total * tile for n in range(len(shares) + 1)]
    return [(start, stop) for start, stop in zip(edges[:-1], edges[1:]) if stop > start]


def kernel_last(scales, point_scale, bias_scale, low_ref, high_ref, top_ref, mix_ref, point_ref, out_ref):
    channels = mix_ref.shape[2]
    half = low_ref.shape[0]
    total = jnp.zeros(point_ref.shape, F32)
    for level, (power, factor) in enumerate(scales):
        at = level * channels
        if at + channels <= half:
            raw = low_ref[at : at + channels]
        elif half <= at < 2 * half:
            raw = high_ref[at - half : at - half + channels]
        else:
            raw = top_ref[at - 2 * half : at - 2 * half + channels]
        raw = raw * power
        total = total + raw
        mix_ref[level] = (raw * factor).astype(BF)
    point_ref[...] = (total * point_scale).astype(BF)
    out_ref[...] = (top_ref[top_ref.shape[0] - 8 : top_ref.shape[0] - 7] * bias_scale).astype(BF)


def shards(fields, cotangent, point_weight, mix_weight, bias_vec):
    rows, columns, channels = fields.shape
    depth = rows.bit_length() - 1
    device_count = lax.axis_size("gx")
    cross_depth = device_count.bit_length() - 1
    levels = depth + cross_depth
    bits = (lax.axis_index("gx") >> jnp.arange(cross_depth, dtype=jnp.int32)) & 1
    flags = jnp.broadcast_to(bits.astype(F32)[:, None], (cross_depth, channels))
    tile = min(TILE, columns)
    tiles = columns // tile

    def params(grant):
        return pltpu.CompilerParams(vmem_limit_bytes=grant * MIB)

    shape = (rows, columns, channels)
    kept = pltpu.VMEM(shape, BF)
    DMA = pltpu.SemaphoreType.DMA
    weight_scratch = pltpu.VMEM((depth, channels, channels), BF)
    mixed_scratch = pltpu.VMEM((rows, tile, channels), F32)
    wide = min(WIDE, columns)
    wide_scratch = pltpu.VMEM((rows, wide, channels), F32)

    def cost(passes, width, products):
        return pl.CostEstimate(
            flops=2 * products * rows * width * channels * channels,
            bytes_accessed=passes * 2 * rows * width * channels,
            transcendentals=0,
        )

    powers = [2.0 ** -(level + 1) for level in range(levels)] + [2.0**-levels]
    scale = jnp.array(powers[depth:], F32)[:, None, None]
    joined_f = (mix_weight[depth:].astype(F32) + point_weight.astype(F32)) * scale
    joined = joined_f.astype(BF)
    joined_back = (joined_f * UNIT).astype(BF)

    coarse, flags = pl.pallas_call(
        functools.partial(kernel_sum, tile),
        in_specs=[VMEM, VMEM],
        out_specs=[VMEM] * 2,
        out_shape=[
            jax.ShapeDtypeStruct((columns, channels), F32),
            jax.ShapeDtypeStruct((cross_depth, channels), F32),
        ],
        compiler_params=params(12),
        cost_estimate=cost(1, columns, 0),
    )(fields, flags)
    core = is_upper(flags, 0)
    count_up = cross_depth - 1
    old = []
    ranges = pieces(columns, wide, [1] * cross_depth)

    def beside_a(n, token):
        if not 0 <= n < len(ranges):
            return 0.0
        start, stop = ranges[n]
        kernel = functools.partial(kernel_a, depth, wide, start, stop)
        if not old:
            kernel = functools.partial(first_call, kernel, 4, 2)
        coeffs, partial, zero = pl.pallas_call(
            kernel,
            in_specs=[VMEM, VMEM, VMEM, HBM] + [VMEM] * len(old),
            out_specs=[VMEM] * 3,
            out_shape=[kept, kept, jax.ShapeDtypeStruct((1, channels), F32)],
            input_output_aliases={4: 0, 5: 1} if old else {},
            scratch_shapes=[weight_scratch, wide_scratch],
            compiler_params=params(12),
            cost_estimate=cost(3, stop - start, 1),
        )(fields, mix_weight, point_weight, token, *old)
        old[:] = [coeffs, partial]
        return zero

    unused_block, coeffs_up = climb(coarse, flags, cross_depth, None, lambda n, token: beside_a(n - 1, token))
    coeffs_up_b = [c.astype(BF) for c in coeffs_up]
    mine, others = cross_mix(coeffs_up_b, joined, flags, False)
    width = columns // 2
    message = jnp.concatenate([others] + coeffs_up[:count_up])
    got = swap(message, 1)
    beside_a(count_up, message)
    coeffs, partial = old
    base = (join(core, mine, got[:width]) + bias_vec.astype(F32)) * STRETCH
    upper = jnp.stack([
        (join(core, coeffs_up[n], got[(n + 1) * width : (n + 2) * width]) * (2.0 * flags[n : n + 1] - 1.0)).astype(BF)
        for n in range(count_up)
    ])

    back, slope_coarse, grads = pl.pallas_call(
        functools.partial(kernel_b, depth, wide),
        in_specs=[VMEM] * 5,
        out_specs=[VMEM] * 3,
        out_shape=[
            kept,
            jax.ShapeDtypeStruct((columns, channels), F32),
            jax.ShapeDtypeStruct((depth + count_up, channels, channels), F32),
        ],
        compiler_params=params(12),
        cost_estimate=cost(4, columns, 1),
    )(partial, cotangent, base, coeffs, upper)

    block, slope_up = climb(slope_coarse, flags, cross_depth, grads.reshape(-1, channels))
    slope_up_b = [c.astype(BF) for c in slope_up]
    mine, others = cross_mix(slope_up_b, joined_back, flags, True)
    back_base = join(core, mine, swap(others, 1))

    ranges = pieces(columns, tile, [3, 5] if cross_depth == 4 else [1] * (cross_depth - 1))
    results = []

    def beside(n, token):
        if n >= len(ranges):
            return 0
        start, stop = ranges[n]
        kernel = functools.partial(kernel_c, depth, tile, start, stop)
        if not results:
            kernel = functools.partial(first_call, kernel, 5, 1)
        grad_input, zero = pl.pallas_call(
            kernel,
            in_specs=[VMEM, VMEM, VMEM, VMEM, HBM] + [HBM] * len(results),
            out_specs=[HBM, VMEM],
            out_shape=[jax.ShapeDtypeStruct(shape, BF), jax.ShapeDtypeStruct((1, channels), F32)],
            input_output_aliases={5: 0} if results else {},
            scratch_shapes=[
                pltpu.VMEM((rows, stop - start, channels), BF), weight_scratch, mixed_scratch, DMA(((stop - start) // tile,))
            ],
            compiler_params=params(12),
            cost_estimate=cost(2, stop - start, 1),
        )(back, back_base, mix_weight, point_weight, token, *results)
        results[:] = [grad_input]
        return zero

    outer = functools.partial(jnp.einsum, "yc,yd->cd", preferred_element_type=F32)
    top = jnp.concatenate(
        [outer(c, b) for c, b in zip(coeffs_up_b[-2:], slope_up_b[-2:])]
        + [jnp.broadcast_to(jnp.sum(slope_up[-1], axis=0, keepdims=True), (8, channels))]
    )
    for degree in reversed(range(1, cross_depth)):
        other = swap(block, 1 << degree)
        zero = beside(cross_depth - 2 - degree, block) if degree < cross_depth - 1 else 0.0
        block = join(is_upper(flags + zero, degree), block, other)
    other = swap(jnp.concatenate([block, top]), 1)
    beside(cross_depth - 2, block)
    half = block.shape[0]
    low, high = jnp.where(core, other[:half], block), jnp.where(core, block, other[:half])
    top = top + other[half:]
    grad_input = results[0]

    global_rows = rows * device_count
    counts = [columns * global_rows / 2 ** (level + 1) for level in range(levels)] + [columns]
    scales = [(power * UNIT, 1.0 / math.sqrt(value)) for power, value in zip(powers, counts)]
    scale_all = 1.0 / math.sqrt(global_rows * columns)
    grad_mix, grad_point, grad_bias = pl.pallas_call(
        functools.partial(kernel_last, scales, scale_all, UNIT * scale_all),
        in_specs=[VMEM] * 3,
        out_specs=[VMEM] * 3,
        out_shape=[
            jax.ShapeDtypeStruct(mix_weight.shape, BF),
            jax.ShapeDtypeStruct(point_weight.shape, BF),
            jax.ShapeDtypeStruct((1, channels), BF),
        ],
        compiler_params=params(12),
    )(low, high, top)
    return (grad_input, grad_mix, grad_point, grad_bias.reshape(channels))


def first_call(kernel, at, count, *refs):
    kernel(*refs[:at], *[None] * count, *refs[at:])


def solution(mesh):
    in_specs = (P("gx", "ga", None), P("gx", "ga", None), P(), P(), P())
    out_specs = (P("gx", "ga", None), P("ga", None, None), P("ga", None), P("ga"))
    return jax.shard_map(shards, mesh=mesh, in_specs=in_specs, out_specs=out_specs, check_vma=False)
```

```python
import functools
import math

import jax
import jax.numpy as jnp
from jax import lax
from jax.experimental import pallas as pl
from jax.experimental.pallas import tpu as pltpu
from jax.sharding import PartitionSpec as P

BF = jnp.bfloat16
F32 = jnp.float32
TILE = 32
WIDE = 64
HBM = pl.BlockSpec(memory_space=pltpu.HBM)
VMEM = pl.BlockSpec(memory_space=pltpu.VMEM)
MIB = 1024 * 1024

GELU_A = math.sqrt(2.0 / math.pi)
GELU_B = 0.044715
STRETCH = math.sqrt(1.5 * GELU_B)
KAPPA = GELU_A * GELU_B / STRETCH**3
UNIT = 1.5 * KAPPA
OFFSET = 1.0 / (3.0 * KAPPA)


def level_starts(depth):
    rows = 1 << depth
    starts, at = [], 0
    for level in range(depth):
        starts.append(at)
        at += rows >> (level + 1)
    return starts


def forward_tree(leaf, put, low, depth, starts):
    half = 1 << (depth - 1)
    row = starts[depth - 1] + (low >> depth)
    if depth == 1:
        even, odd = leaf(low), leaf(low + 1)
        put(0, row, odd - even)
        return even.astype(F32) + odd.astype(F32)
    even = forward_tree(leaf, put, low, depth - 1, starts)
    odd = forward_tree(leaf, put, low + half, depth - 1, starts)
    put(depth - 1, row, (odd - even).astype(BF))
    return even + odd


def inverse_tree(take, leaf, low, depth, starts, value):
    if depth == 0:
        leaf(low, value)
        return
    half = 1 << (depth - 1)
    detail = take(starts[depth - 1] + (low >> depth))
    inverse_tree(take, leaf, low, depth - 1, starts, value - detail)
    inverse_tree(take, leaf, low + half, depth - 1, starts, value + detail)


def join_weights(mix_ref, point_ref, joined_ref, unit):
    point = point_ref[...].astype(F32)
    for level in range(joined_ref.shape[0]):
        joined_ref[level] = ((mix_ref[level].astype(F32) + point) * (unit * 2.0 ** -(level + 1))).astype(BF)


def mix_details(coeffs_ref, weight_ref, mixed_ref, columns, depth, starts, back):
    tile, channels = mixed_ref.shape[1:]
    for level in range(depth):
        count = 1 << (depth - 1 - level)
        span = slice(starts[level], starts[level] + count)
        left = coeffs_ref[span, columns].reshape(count * tile, channels)
        dims = (((1,), (1 if back else 0,)), ((), ()))
        mixed = lax.dot_general(left, weight_ref[level], dims, preferred_element_type=F32)
        mixed_ref[span] = mixed.reshape(count, tile, channels)


def tile_span(index, tile, first=0):
    return pl.ds(pl.multiple_of(first + index * tile, tile), tile)


def kernel_sum(tile, fields_v, flags_ref, out_ref, flags_out):
    flags_out[...] = flags_ref[...]
    rows, columns = fields_v.shape[:2]

    def step(index, unused):
        here = tile_span(index, tile)
        total = fields_v[0, here].astype(F32)
        for row in range(1, rows):
            total = total + fields_v[row, here].astype(F32)
        out_ref[here] = total
        return 0

    lax.fori_loop(0, columns // tile, step, 0)


def kernel_a(depth, tile, first, stop, fields_v, mix_ref, point_ref, token_ref, old_c, old_p,
             coeffs_v, partial_v, done_ref, weight_ref, mixed_ref):
    starts = level_starts(depth)
    zero = jnp.zeros(mixed_ref.shape[1:], F32)
    done_ref[...] = jnp.zeros_like(done_ref)
    join_weights(mix_ref, point_ref, weight_ref, 1.0)

    def step(index, unused):
        here = tile_span(index, tile, first)

        def put(level, row, value):
            coeffs_v[row, here] = value

        forward_tree(lambda row: fields_v[row, here], put, 0, depth, starts)
        mix_details(coeffs_v, weight_ref, mixed_ref, here, depth, starts, False)

        def leaf(row, value):
            partial_v[row, here] = (value * STRETCH).astype(BF)

        inverse_tree(lambda row: mixed_ref[row], leaf, 0, depth, starts, zero)
        return 0

    lax.fori_loop(0, (stop - first) // tile, step, 0)


def kernel_b(depth, tile, partial_v, cot_v, base_ref, coeffs_v, upper_ref, back_v, coarse_ref, grads_ref):
    starts = level_starts(depth)
    columns, channels = base_ref.shape
    group = max(1, 256 // tile)

    grads_ref[...] = jnp.zeros_like(grads_ref)
    outer = functools.partial(
        lax.dot_general, dimension_numbers=(((0,), (0,)), ((), ())), preferred_element_type=F32
    )

    def step(index, unused):
        here = tile_span(index, tile)
        base = base_ref[here]
        waiting = [[] for _ in range(depth)]

        def leaf(row):
            y = partial_v[row, here].astype(F32) + base
            x = y * (y * y + 1.5)
            t = jnp.tanh(KAPPA * x)
            slope = (1.0 + t) * (OFFSET + (x - y) * (1.0 - t))
            return slope.astype(BF) * cot_v[row, here]

        def put(level, row, value):
            back_v[row, here] = value
            held = waiting[level]
            held.append(value)
            size = len(held)
            if size == group or row + 1 == starts[level] + (1 << (depth - 1 - level)):
                right = jnp.stack(held).reshape(size * tile, channels)
                left = coeffs_v[row + 1 - size : row + 1, here].reshape(size * tile, channels)
                grads_ref[level] += outer(left, right)
                held.clear()

        coarse_ref[here] = forward_tree(leaf, put, 0, depth, starts)
        return 0

    lax.fori_loop(0, columns // tile, step, 0)
    coarse = coarse_ref[...]
    high = coarse.astype(BF)
    low = (coarse - high.astype(F32)).astype(BF)
    for n in range(upper_ref.shape[0]):
        grads_ref[depth + n] = outer(upper_ref[n], high) + outer(upper_ref[n], low)


def kernel_c(depth, tile, first, stop, back_v, base_ref, mix_ref, point_ref, token_ref, old_out, out_ref, done_ref,
             out_v, weight_ref, mixed_ref, sems):
    starts = level_starts(depth)
    count = (stop - first) // tile
    done_ref[...] = jnp.zeros_like(done_ref)
    join_weights(mix_ref, point_ref, weight_ref, UNIT)

    def copy(index):
        here = tile_span(index, tile)
        return pltpu.make_async_copy(
            out_v.at[:, here], out_ref.at[:, tile_span(index, tile, first)], sems.at[index]
        )

    def step(index, unused):
        here = tile_span(index, tile)
        there = tile_span(index, tile, first)
        mix_details(back_v, weight_ref, mixed_ref, there, depth, starts, True)

        def leaf(row, value):
            out_v[row, here] = value.astype(BF)

        inverse_tree(lambda row: mixed_ref[row], leaf, 0, depth, starts, base_ref[there])
        copy(index).start()
        return 0

    lax.fori_loop(0, count, step, 0)
    for index in range(count):
        copy(index).wait()


def swap(block, stride):
    count = lax.axis_size("gx")
    return lax.ppermute(block, "gx", [(low, low ^ stride) for low in range(count)])


def is_upper(flags, degree):
    return flags[degree : degree + 1] > 0.5


def mix_row(coeffs_b, weight, back):
    spec = "yc,dc->yd" if back else "yc,cd->yd"
    return jnp.einsum(spec, coeffs_b, weight, preferred_element_type=F32)


def cross_mix(coeffs_b, weights, flags, back):
    total = mix_row(coeffs_b[-1], weights[-1], back)
    for degree in reversed(range(1, len(coeffs_b) - 1)):
        part = mix_row(coeffs_b[degree], weights[degree], back)
        total = total + jnp.where(is_upper(flags, degree), part, -part)
    part = mix_row(coeffs_b[0], weights[0], back)
    return pick(is_upper(flags, 0), total - part, total + part)


def pick(upper, low, high):
    return jnp.where(upper, high, low), jnp.where(upper, low, high)


def join(upper, mine, other):
    return jnp.where(upper, jnp.concatenate([other, mine]), jnp.concatenate([mine, other]))


def climb(coarse, flags, depth, block=None, beside=None):
    found = []
    columns = coarse.shape[0] // 2
    for degree in range(depth):
        upper = is_upper(flags, degree)
        send = coarse
        if degree == 0:
            coarse, send = pick(upper, coarse[:columns], coarse[columns:])
        other = half = None
        if block is not None:
            half = block.shape[0] // 2
            keep, gone = pick(upper, block[:half], block[half:])
            send = jnp.concatenate([gone, send])
        other = swap(send, 1 << degree)
        if block is not None:
            block, other = keep + other[:half], other[half:]
        found.append(jnp.where(upper, coarse - other, other - coarse))
        coarse = coarse + other
        if beside is not None:
            coarse = coarse + beside(degree, send)
    return block, found + [coarse]


def pieces(columns, tile, shares):
    tiles = columns // tile
    total = sum(shares)
    edges = [tiles * sum(shares[:n]) // total * tile for n in range(len(shares) + 1)]
    return [(start, stop) for start, stop in zip(edges[:-1], edges[1:]) if stop > start]


def kernel_last(scales, point_scale, bias_scale, low_ref, high_ref, top_ref, mix_ref, point_ref, out_ref):
    channels = mix_ref.shape[2]
    half = low_ref.shape[0]
    total = jnp.zeros(point_ref.shape, F32)
    for level, (power, factor) in enumerate(scales):
        at = level * channels
        if at + channels <= half:
            raw = low_ref[at : at + channels]
        elif half <= at < 2 * half:
            raw = high_ref[at - half : at - half + channels]
        else:
            raw = top_ref[at - 2 * half : at - 2 * half + channels]
        raw = raw * power
        total = total + raw
        mix_ref[level] = (raw * factor).astype(BF)
    point_ref[...] = (total * point_scale).astype(BF)
    out_ref[...] = (top_ref[top_ref.shape[0] - 8 : top_ref.shape[0] - 7] * bias_scale).astype(BF)


def shards(fields, cotangent, point_weight, mix_weight, bias_vec):
    rows, columns, channels = fields.shape
    depth = rows.bit_length() - 1
    device_count = lax.axis_size("gx")
    cross_depth = device_count.bit_length() - 1
    levels = depth + cross_depth
    bits = (lax.axis_index("gx") >> jnp.arange(cross_depth, dtype=jnp.int32)) & 1
    flags = jnp.broadcast_to(bits.astype(F32)[:, None], (cross_depth, channels))
    tile = min(TILE, columns)
    tiles = columns // tile

    def params(grant):
        return pltpu.CompilerParams(vmem_limit_bytes=grant * MIB)

    shape = (rows, columns, channels)
    kept = pltpu.VMEM(shape, BF)
    DMA = pltpu.SemaphoreType.DMA
    weight_scratch = pltpu.VMEM((depth, channels, channels), BF)
    mixed_scratch = pltpu.VMEM((rows, tile, channels), F32)
    wide = min(WIDE, columns)
    wide_scratch = pltpu.VMEM((rows, wide, channels), F32)

    def cost(passes, width, products):
        return pl.CostEstimate(
            flops=2 * products * rows * width * channels * channels,
            bytes_accessed=passes * 2 * rows * width * channels,
            transcendentals=0,
        )

    powers = [2.0 ** -(level + 1) for level in range(levels)] + [2.0**-levels]
    scale = jnp.array(powers[depth:], F32)[:, None, None]
    joined_f = (mix_weight[depth:].astype(F32) + point_weight.astype(F32)) * scale
    joined = joined_f.astype(BF)
    joined_back = (joined_f * UNIT).astype(BF)

    coarse, flags = pl.pallas_call(
        functools.partial(kernel_sum, min(2 * WIDE, columns)),
        in_specs=[VMEM, VMEM],
        out_specs=[VMEM] * 2,
        out_shape=[
            jax.ShapeDtypeStruct((columns, channels), F32),
            jax.ShapeDtypeStruct((cross_depth, channels), F32),
        ],
        compiler_params=params(12),
        cost_estimate=cost(1, columns, 0),
    )(fields, flags)
    core = is_upper(flags, 0)
    count_up = cross_depth - 1
    old = []
    ranges = pieces(columns, wide, [1] * cross_depth)

    def beside_a(n, token):
        if not 0 <= n < len(ranges):
            return 0.0
        start, stop = ranges[n]
        kernel = functools.partial(kernel_a, depth, wide, start, stop)
        if not old:
            kernel = functools.partial(first_call, kernel, 4, 2)
        coeffs, partial, zero = pl.pallas_call(
            kernel,
            in_specs=[VMEM, VMEM, VMEM, HBM] + [VMEM] * len(old),
            out_specs=[VMEM] * 3,
            out_shape=[kept, kept, jax.ShapeDtypeStruct((1, channels), F32)],
            input_output_aliases={4: 0, 5: 1} if old else {},
            scratch_shapes=[weight_scratch, wide_scratch],
            compiler_params=params(12),
            cost_estimate=cost(3, stop - start, 1),
        )(fields, mix_weight, point_weight, token, *old)
        old[:] = [coeffs, partial]
        return zero

    unused_block, coeffs_up = climb(coarse, flags, cross_depth, None, lambda n, token: beside_a(n - 1, token))
    coeffs_up_b = [c.astype(BF) for c in coeffs_up]
    mine, others = cross_mix(coeffs_up_b, joined, flags, False)
    width = columns // 2
    message = jnp.concatenate([others] + coeffs_up[:count_up])
    got = swap(message, 1)
    beside_a(count_up, message)
    coeffs, partial = old
    base = (join(core, mine, got[:width]) + bias_vec.astype(F32)) * STRETCH
    upper = jnp.stack([
        (join(core, coeffs_up[n], got[(n + 1) * width : (n + 2) * width]) * (2.0 * flags[n : n + 1] - 1.0)).astype(BF)
        for n in range(count_up)
    ])

    back, slope_coarse, grads = pl.pallas_call(
        functools.partial(kernel_b, depth, wide),
        in_specs=[VMEM] * 5,
        out_specs=[VMEM] * 3,
        out_shape=[
            kept,
            jax.ShapeDtypeStruct((columns, channels), F32),
            jax.ShapeDtypeStruct((depth + count_up, channels, channels), F32),
        ],
        compiler_params=params(12),
        cost_estimate=cost(4, columns, 1),
    )(partial, cotangent, base, coeffs, upper)

    block, slope_up = climb(slope_coarse, flags, cross_depth, grads.reshape(-1, channels))
    slope_up_b = [c.astype(BF) for c in slope_up]
    mine, others = cross_mix(slope_up_b, joined_back, flags, True)
    back_base = join(core, mine, swap(others, 1))

    ranges = pieces(columns, tile, [3, 5] if cross_depth == 4 else [1] * (cross_depth - 1))
    results = []

    def beside(n, token):
        if n >= len(ranges):
            return 0
        start, stop = ranges[n]
        kernel = functools.partial(kernel_c, depth, tile, start, stop)
        if not results:
            kernel = functools.partial(first_call, kernel, 5, 1)
        grad_input, zero = pl.pallas_call(
            kernel,
            in_specs=[VMEM, VMEM, VMEM, VMEM, HBM] + [HBM] * len(results),
            out_specs=[HBM, VMEM],
            out_shape=[jax.ShapeDtypeStruct(shape, BF), jax.ShapeDtypeStruct((1, channels), F32)],
            input_output_aliases={5: 0} if results else {},
            scratch_shapes=[
                pltpu.VMEM((rows, stop - start, channels), BF), weight_scratch, mixed_scratch, DMA(((stop - start) // tile,))
            ],
            compiler_params=params(12),
            cost_estimate=cost(2, stop - start, 1),
        )(back, back_base, mix_weight, point_weight, token, *results)
        results[:] = [grad_input]
        return zero

    outer = functools.partial(jnp.einsum, "yc,yd->cd", preferred_element_type=F32)
    top = jnp.concatenate(
        [outer(c, b) for c, b in zip(coeffs_up_b[-2:], slope_up_b[-2:])]
        + [jnp.broadcast_to(jnp.sum(slope_up[-1], axis=0, keepdims=True), (8, channels))]
    )
    for degree in reversed(range(1, cross_depth)):
        other = swap(block, 1 << degree)
        zero = beside(cross_depth - 2 - degree, block) if degree < cross_depth - 1 else 0.0
        block = join(is_upper(flags + zero, degree), block, other)
    other = swap(jnp.concatenate([block, top]), 1)
    beside(cross_depth - 2, block)
    half = block.shape[0]
    low, high = jnp.where(core, other[:half], block), jnp.where(core, block, other[:half])
    top = top + other[half:]
    grad_input = results[0]

    global_rows = rows * device_count
    counts = [columns * global_rows / 2 ** (level + 1) for level in range(levels)] + [columns]
    scales = [(power * UNIT, 1.0 / math.sqrt(value)) for power, value in zip(powers, counts)]
    scale_all = 1.0 / math.sqrt(global_rows * columns)
    grad_mix, grad_point, grad_bias = pl.pallas_call(
        functools.partial(kernel_last, scales, scale_all, UNIT * scale_all),
        in_specs=[VMEM] * 3,
        out_specs=[VMEM] * 3,
        out_shape=[
            jax.ShapeDtypeStruct(mix_weight.shape, BF),
            jax.ShapeDtypeStruct(point_weight.shape, BF),
            jax.ShapeDtypeStruct((1, channels), BF),
        ],
        compiler_params=params(12),
    )(low, high, top)
    return (grad_input, grad_mix, grad_point, grad_bias.reshape(channels))


def first_call(kernel, at, count, *refs):
    kernel(*refs[:at], *[None] * count, *refs[at:])


def solution(mesh):
    in_specs = (P("gx", "ga", None), P("gx", "ga", None), P(), P(), P())
    out_specs = (P("gx", "ga", None), P("ga", None, None), P("ga", None), P("ga"))
    return jax.shard_map(shards, mesh=mesh, in_specs=in_specs, out_specs=out_specs, check_vma=False)
```
